512 devices in a mesh: inner: 16 (over z, x_lo), outer: 32 (over y, x_hi, core).
Axes of the slice: x: 4 (x_hi: 2, x_lo: 2; x = x_hi * 2 + x_lo), y: 8, z: 8, core: 2. Of those that a mesh axis runs over, the one named last changes fastest.
Arguments:
- points: bfloat16 [32, 4096, 1024], P('outer', 'inner'), may hold values from -6 to 6
- anchor_index: int32 [32, 2048], P('outer', 'inner'), may hold values from 0 to 255
- norm_gain: float32 [1024], replicated, may hold values from 0.1 to 1.9
- weight_mean: bfloat16 [1024, 1536], P('outer'), may hold values from -0.25 to 0.25
- weight_scale: float32 [1536], replicated, may hold values from 0.01 to 0.04
- noise_seed: int32 [1536], replicated, may hold values from 0 to 16777215
- out_weight: bfloat16 [512, 1024], P('outer'), may hold values from -0.75 to 0.75
- cotangent: bfloat16 [32, 2048, 1024], P('outer', 'inner'), may hold values from -6 to 6
Outputs:
- attended: bfloat16 [32, 2048, 1024], P('outer', 'inner')
- grad_points: float32 [32, 4096, 1024], P('outer', 'inner')
- grad_scale: float32 [1536], replicated
The draws below stay inside these ranges and needn't reach their ends.
All inputs are finite; a program needn't handle non-finite values.
Results may differ from the reference program's by a relative error of at most 0.022.
The reference program's roundings to bfloat16 on the way count: a program that leaves them out, or rounds other values in their place, can miss the bound.
Values may be sent and summed in bfloat16 or wider, within the bound.
A program may use at most 64 MiB of HBM per device.

```python
import math
import jax
import jax.numpy as jnp
from jax import lax

D = 1024
HEADS = 8
HEAD_DIM = 64
HD = 512
TOK_DEV = 128
PTS_DEV = 256
SAMPLES = 32
LENGTH = 2048
POINTS = 4096
N_INNER = 16


def touch_ends(entries, rng, least, top_value):
    place = [jax.random.randint(jax.random.fold_in(rng, axis), (), 0, length) for axis, length in enumerate(entries.shape)]
    widest = entries.shape.index(max(entries.shape))
    beside = place[:widest] + [(place[widest] + 1) % entries.shape[widest]] + place[widest + 1:]
    return entries.at[tuple(place)].set(least).at[tuple(beside)].set(top_value)


def block_scale(own_key, extent, pieces, smallest, largest):
    factor_of = 1.0
    for dim, parts in pieces:
        draws = jax.random.uniform(jax.random.fold_in(jax.random.fold_in(own_key, 6), dim), (parts,), jnp.float32, smallest / len(pieces), largest / len(pieces))
        factor_of = factor_of * jnp.repeat(jnp.exp(draws), extent[dim] // parts).reshape((-1,) + (1,) * (len(extent) - 1 - dim))
    return factor_of


def gaussian(own_key, shape, deviation, reach, split=(), held_as=jnp.bfloat16):
    entries = jax.random.normal(own_key, shape, jnp.float32) * deviation
    if len(split) > 0:
        entries = block_scale(own_key, shape, split, -0.22, 0.18) * entries
    return jnp.clip(entries, min=-reach, max=reach).astype(held_as)


def setup_inputs(seed: int = 0) -> dict:
    key_of = jax.random.split(jax.random.key(seed), 9)
    return {
        "points": gaussian(key_of[0], (SAMPLES, POINTS, D), 1.0, 6.0, ((0, 32), (1, 16))),
        "anchor_index": touch_ends(jax.random.randint(key_of[1], (SAMPLES, LENGTH), 0, PTS_DEV), jax.random.fold_in(key_of[1], 1), 0, PTS_DEV - 1).astype(jnp.int32),
        "norm_gain": jnp.clip(1.0 + 0.18 * jax.random.normal(key_of[2], (D,), jnp.float32), 0.1, 1.9),
        "weight_mean": gaussian(key_of[3], (D, 3 * HD), (D // 2) ** -0.5, 0.25, ((0, 32),)),
        "weight_scale": jnp.clip(jnp.exp(jax.random.uniform(key_of[4], (3 * HD,), jnp.float32, math.log(0.01), math.log(0.04))), 0.01, 0.04),
        "noise_seed": touch_ends(jax.random.randint(key_of[5], (3 * HD,), 0, 16777216), jax.random.fold_in(key_of[5], 1), 0, 16777215).astype(jnp.int32),
        "out_weight": gaussian(key_of[6], (HD, D), (HD // 8) ** -0.5, 0.75, ((0, 32),)),
        "cotangent": gaussian(key_of[7], (SAMPLES, LENGTH, D), 1.0, 6.0, ((0, 32), (1, 16))),
    }


def hashed_noise(seeds, row_count):
    row_ids = jnp.arange(row_count, dtype=jnp.int32)[:, None]
    hashed = seeds[None, :] * 747796405 + row_ids * 1103515245 + 12345
    hashed = hashed ^ hashed >> 15 & 131071
    hashed = hashed * 277803737
    hashed = hashed ^ hashed >> 16 & 65535
    fraction = (hashed >> 8 & 65535).astype(jnp.float32) / 65536.0 + 1.0 / 131072.0
    return (fraction - 0.5) * 3.4641016

def rms_normalize(values, norm_gain):
    mean_square = lax.optimization_barrier(jnp.mean(values * values, axis=-1, keepdims=True))
    return values * lax.rsqrt(mean_square + 1e-06) * norm_gain

def rounded(values):
    return lax.optimization_barrier(values.astype(jnp.bfloat16)).astype(jnp.float32)

def one_sample(sample_points, sample_index, sample_cotangent, norm_gain, weight_full, out_weight, noise):
    score_scale = HEAD_DIM ** (-0.5)
    value_width = HEADS * HEAD_DIM
    offsets = jnp.arange(LENGTH, dtype=jnp.int32) // TOK_DEV * PTS_DEV
    picked = (offsets + sample_index).astype(jnp.int32)
    anchors = jnp.take(sample_points, picked, axis=0)
    anchors_f = anchors.astype(jnp.float32)
    normed = rms_normalize(anchors_f, norm_gain).astype(jnp.bfloat16)
    projected = jnp.dot(normed, weight_full, preferred_element_type=jnp.float32).astype(jnp.bfloat16)
    projected_f = projected.astype(jnp.float32)
    query_h = projected_f[:, :value_width].reshape(LENGTH, HEADS, HEAD_DIM)
    key_h = projected_f[:, value_width:2 * value_width].reshape(LENGTH, HEADS, HEAD_DIM)
    value_h = projected_f[:, 2 * value_width:].reshape(LENGTH, HEADS, HEAD_DIM)
    scores = jnp.einsum('qhd,khd->hqk', query_h, key_h) * score_scale
    weights = jnp.exp(scores)
    totals = lax.optimization_barrier(jnp.sum(weights, axis=-1))
    summed = jnp.einsum('hqk,khd->qhd', rounded(weights), value_h)
    attention = (summed / totals.T[:, :, None]).astype(jnp.bfloat16).reshape(LENGTH, value_width)
    attended = jnp.dot(attention, out_weight, preferred_element_type=jnp.float32).astype(jnp.bfloat16)
    grad_attention = jnp.dot(sample_cotangent, out_weight.T, preferred_element_type=jnp.float32).astype(jnp.bfloat16)
    grad_h = grad_attention.astype(jnp.float32).reshape(LENGTH, HEADS, HEAD_DIM)
    attention_h = attention.astype(jnp.float32).reshape(LENGTH, HEADS, HEAD_DIM)
    delta = lax.optimization_barrier(jnp.sum(grad_h * attention_h, axis=-1))
    probs = weights / totals[:, :, None]
    grad_probs = jnp.einsum('qhd,khd->hqk', grad_h, value_h)
    grad_scores = rounded(probs * (grad_probs - delta.T[:, :, None]))
    grad_query = jnp.einsum('hqk,khd->qhd', grad_scores, key_h) * score_scale
    block_scores = grad_scores.reshape(HEADS, N_INNER, TOK_DEV, LENGTH)
    block_probs = rounded(probs).reshape(HEADS, N_INNER, TOK_DEV, LENGTH)
    block_query = query_h.reshape(N_INNER, TOK_DEV, HEADS, HEAD_DIM)
    block_grad = grad_h.reshape(N_INNER, TOK_DEV, HEADS, HEAD_DIM)
    key_parts = rounded(jnp.einsum('hbqk,bqhd->bkhd', block_scores, block_query) * score_scale)
    value_parts = rounded(jnp.einsum('hbqk,bqhd->bkhd', block_probs, block_grad))
    grad_keys = lax.optimization_barrier(jnp.sum(key_parts, axis=0)).reshape(LENGTH, value_width)
    grad_values = lax.optimization_barrier(jnp.sum(value_parts, axis=0)).reshape(LENGTH, value_width)
    grad_projected = jnp.concatenate([grad_query.reshape(LENGTH, value_width), grad_keys, grad_values], axis=1).astype(jnp.bfloat16)
    grad_normed = jnp.dot(grad_projected, weight_full.T, preferred_element_type=jnp.float32)
    weight_grad = jnp.dot(normed.T, grad_projected, preferred_element_type=jnp.float32)
    scale_part = lax.optimization_barrier(jnp.sum(weight_grad * noise, axis=0))
    pullback = jax.vjp(lambda values: rms_normalize(values, norm_gain), anchors_f)[1]
    grad_anchors = pullback(grad_normed)[0]
    grad_points = jnp.zeros((PTS_DEV * N_INNER, D), jnp.float32).at[picked].add(grad_anchors)
    return (attended, grad_points, scale_part)

def reference(points, anchor_index, norm_gain, weight_mean, weight_scale, noise_seed, out_weight, cotangent):
    noise = hashed_noise(noise_seed, D)
    weight_full = (weight_mean.astype(jnp.float32) + weight_scale[None, :] * noise).astype(jnp.bfloat16)

    def per_sample(items):
        return one_sample(items[0], items[1], items[2], norm_gain, weight_full, out_weight, noise)
    attended, grad_points, scale_parts = lax.map(per_sample, (points, anchor_index, cotangent))
    return (attended, grad_points, lax.optimization_barrier(jnp.sum(scale_parts, axis=0)))
```

```python
import functools

import jax
import jax.numpy as jnp
from jax import lax
from jax.experimental import pallas as pl
from jax.experimental.pallas import tpu as pltpu
from jax.sharding import PartitionSpec as P

MESH = pl.DeviceIdType.MESH
BF = jnp.bfloat16
F32 = jnp.float32

HEADS = 8
TOK = 128
PTS = 256
D = 1024
HD = 512
NZ = 8
NY = 8
LOG2E = 1.4426950408889634

KV, Q, O = 0, 1, 2
M_KV, M_Q, M_G, M_ATT, M_DQ, M_DKV = range(6)


def left_half(rows):
    return lax.broadcasted_iota(jnp.int32, (rows, 128), 1) < 64


def swap(x):
    return pltpu.roll(x, 64, 1)


def dot(a, b):
    return jnp.dot(a, b, preferred_element_type=F32)


def dot_nt(a, b):
    return lax.dot_general(a, b, (((1,), (1,)), ((), ())), preferred_element_type=F32)


def body(
    points_ref,
    idx_ref,
    gain_ref,
    mean_ref,
    scale_ref,
    seed_ref,
    outw_ref,
    cot_ref,
    att_out,
    gp_out,
    gs_out,
    pts,
    cot,
    mean_buf,
    out_buf,
    noise_buf,
    nhi,
    nlo,
    wbuf,
    anch,
    normed,
    ubuf,
    kv_send,
    q_send,
    g_send,
    kv_buf,
    kv1_buf,
    q_buf,
    g_buf,
    qz,
    gz,
    qgt,
    wexp,
    oacc,
    inv_buf,
    del_buf,
    dq_acc,
    dkvt,
    dkv_own,
    dkv_x,
    dkv_sib,
    dkv_send,
    att_send,
    dq_send,
    att_buf,
    dq_buf,
    dkv_buf,
    ps_buf,
    loc_sem,
    ring_s,
    ring_r,
    xh_s,
    xh_r,
    sib_s,
    sib_r,
    a2a_s,
    a2a_r,
    skv_s,
    skv_r,
    sdk_s,
    sdk_r,
    ps_s,
    ps_r,
):
    inner = lax.axis_index("inner")
    outer = lax.axis_index("outer")
    z = inner // 2
    xl = inner % 2
    y = outer // 4
    xh = (outer // 2) % 2
    c = outer % 2

    def dev(z_, xl_, y_, xh_, c_):
        return {"inner": z_ * 2 + xl_, "outer": (y_ * 2 + xh_) * 2 + c_}

    def xgroup(k):
        g = (xl * 4 + xh * 2 + c + k) % 8
        return dev(z, g // 4, y, (g // 2) % 2, g % 2)

    def zpeer(k):
        return dev((z + k) % NZ, xl, y, xh, c)

    def ypeer(k):
        return dev(z, xl, (y + k) % NY, xh, c)

    def rcopy(src, dst, ssem, rsem, to):
        return pltpu.make_async_remote_copy(
            src_ref=src,
            dst_ref=dst,
            send_sem=ssem,
            recv_sem=rsem,
            device_id=to,
            device_id_type=MESH,
        )

    sends = []

    def start(copy):
        copy.start()
        sends.append(copy)

    ld_pts = pltpu.make_async_copy(points_ref, pts, loc_sem.at[0])
    ld_cot = pltpu.make_async_copy(cot_ref, cot, loc_sem.at[1])
    ld_pts.start()
    ld_cot.start()

    diag = xl == c
    bar = pltpu.get_barrier_semaphore()

    def hpeer(k):
        return dev((z + k) % NZ, c, y, xh, xl)

    for k in range(1, 8):
        for to in (xgroup(k), zpeer(k), ypeer(k)):
            pl.semaphore_signal(bar, inc=1, device_id=to, device_id_type=MESH)

    @pl.when(jnp.logical_not(diag))
    def _():
        for k in range(1, 8):
            pl.semaphore_signal(bar, inc=1, device_id=hpeer(k), device_id_type=MESH)

    @pl.when(diag)
    def _():
        pl.semaphore_wait(bar, 21)

    @pl.when(jnp.logical_not(diag))
    def _():
        pl.semaphore_wait(bar, 28)

    own = outer

    def block(part, row):
        if part == KV:
            return mean_buf.at[row, :, pl.ds(HD, 2 * HD)]
        if part == Q:
            return mean_buf.at[row, :, pl.ds(0, HD)]
        return out_buf.at[row]

    def shard_of(delta, r, core):
        return ((y + delta) % NY * 2 + (xh + r) % 2) * 2 + core

    sibling = dev(z, xl, y, xh, 1 - c)
    partner = dev(z, xl, y, 1 - xh, c)
    up, down = ypeer(1), ypeer(7)

    def ring_copy(part, direction, dist, r):
        delta = (8 - (dist - 1)) % 8 if direction == 0 else dist - 1
        b = block(part, shard_of(delta, r, c))
        return rcopy(
            b,
            b,
            ring_s.at[part, direction, dist - 1, r],
            ring_r.at[part, direction, dist - 1, r],
            up if direction == 0 else down,
        )

    def ring_arrival(part, direction, dist, r):
        delta = (8 - dist) % 8 if direction == 0 else dist
        b = block(part, shard_of(delta, r, c))
        rcopy(
            b,
            b,
            ring_s.at[part, direction, dist - 1, r],
            ring_r.at[part, direction, dist - 1, r],
            up,
        ).wait_recv()

    def sib_copy(part, delta, r):
        b = block(part, shard_of(delta, r, c))
        return rcopy(b, b, sib_s.at[part, delta, r], sib_r.at[part, delta, r], sibling)

    def stage_own(part):
        b = block(part, own)
        start(rcopy(b, b, xh_s.at[part], xh_r.at[part], partner))
        start(ring_copy(part, 0, 1, 0))
        start(ring_copy(part, 1, 1, 0))
        start(sib_copy(part, 0, 0))

    def stage_partner(part):
        b = block(part, shard_of(0, 1, c))
        rcopy(b, b, xh_s.at[part], xh_r.at[part], partner).wait_recv()
        start(ring_copy(part, 0, 1, 1))
        start(ring_copy(part, 1, 1, 1))
        start(sib_copy(part, 0, 1))

    def stage_ring(part, dist, r):
        for direction in (0, 1):
            if dist == 4 and direction != r:
                continue
            ring_arrival(part, direction, dist, r)
            if dist < 3 or (dist == 3 and direction == r):
                start(ring_copy(part, direction, dist + 1, r))
            delta = (8 - dist) % 8 if direction == 0 else dist
            start(sib_copy(part, delta, r))

    def stage_last(part):
        stage_ring(part, 4, 0)
        stage_ring(part, 4, 1)

    def stage_sibling(part):
        for delta in range(8):
            for r in (0, 1):
                b = block(part, shard_of(delta, r, 1 - c))
                rcopy(
                    b, b, sib_s.at[part, delta, r], sib_r.at[part, delta, r], sibling
                ).wait_recv()

    mean_buf[own] = mean_ref[...]
    out_buf[own] = outw_ref[...]
    stage_own(KV)

    def make_normed():
        ld_pts.wait()
        sel_t = (
            lax.broadcasted_iota(jnp.int32, (PTS, TOK), 0) == idx_ref[...]
        ).astype(F32)
        a = dot(sel_t.T.astype(BF), pts[...])
        anch[...] = a
        r = lax.rsqrt(jnp.mean(a * a, axis=-1, keepdims=True) + 1e-06)
        normed[...] = (a * r * gain_ref[...]).astype(BF)

    def make_noise(chunk):
        def step(t, carry):
            row = pl.multiple_of(chunk * 128 + t * 16, 16)
            for col in range(0, 3 * HD, HD):
                cols = pl.ds(col, HD)
                ids = lax.broadcasted_iota(jnp.int32, (16, HD), 0) + row
                h = seed_ref[:, cols] * 747796405 + 12345 + ids * 1103515245
                h = h ^ lax.shift_right_logical(h, jnp.full_like(h, 15))
                h = h * 277803737
                h = h ^ lax.shift_right_logical(h, jnp.full_like(h, 16))
                h = lax.shift_right_logical(h, jnp.full_like(h, 8)) & 65535
                n = (h.astype(F32) - 32767.5) * (3.4641016 / 65536.0)
                noise_buf[pl.ds(row, 16), cols] = n
                hi = n.astype(BF)
                nhi[pl.ds(row, 16), cols] = hi
                nlo[pl.ds(row, 16), cols] = (n - hi.astype(F32)).astype(BF)
            return carry

        lax.fori_loop(0, 8, step, 0)

    def make_u(third):
        cols = pl.ds(third * HD, HD)
        x = normed[...]
        ubuf[:, cols] = dot(x, nhi[:, cols]) + dot(x, nlo[:, cols])

    def form_weight(col, width):
        cols = pl.ds(col, width)

        def step(s, carry):
            row = pl.multiple_of(s * 32, 32)
            w = mean_buf[s, :, cols].astype(F32) + scale_ref[:, cols] * noise_buf[
                pl.ds(row, 32), cols
            ]
            wbuf[pl.ds(row, 32), cols] = w.astype(BF)
            return carry

        lax.fori_loop(0, 32, step, 0)

    def rnd(x):
        return x.astype(BF).astype(F32)

    m128 = left_half(128)
    m64 = left_half(64)

    def project_kv():
        x = normed[...]
        for t in range(2):
            k2 = rnd(dot(x, wbuf[:, pl.ds(HD + 256 * t, 256)]))
            v2 = rnd(dot(x, wbuf[:, pl.ds(2 * HD + 256 * t, 256)]))
            for u in range(2):
                k = k2[:, u * 128 : u * 128 + 128]
                v = v2[:, u * 128 : u * 128 + 128]
                h = 4 * t + 2 * u
                kv_send[h] = jnp.where(m128, k, swap(v)).astype(BF)
                kv_send[h + 1] = jnp.where(m128, swap(k), v).astype(BF)

    def pack_pair(x, h, ref):
        top, bot = x[:64], x[64:]
        ref[h] = jnp.where(m64, top, swap(bot)).astype(BF)
        ref[h + 1] = jnp.where(m64, swap(top), bot).astype(BF)

    def project_q():
        x = normed[...]
        for t in range(2):
            q2 = rnd(dot(x, wbuf[:, pl.ds(256 * t, 256)]))
            for u in range(2):
                pack_pair(q2[:, u * 128 : u * 128 + 128], 4 * t + 2 * u, q_send)

    def project_g():
        ld_cot.wait()
        x = cot[...]
        for t in range(2):
            w = out_buf[pl.ds(16 * t, 16)].reshape(256, D)
            g2 = rnd(dot_nt(x, w))
            for u in range(2):
                pack_pair(g2[:, u * 128 : u * 128 + 128], 4 * t + 2 * u, g_send)

    late = (4, 3, 5, 2, 6, 1, 7)

    def a2a_one(msg, src_buf, dst_buf, k):
        there = (z + k) % NZ
        return rcopy(
            src_buf.at[there], dst_buf.at[z], a2a_s.at[msg, k], a2a_r.at[msg, k], hpeer(k)
        )

    def a2a_start(msg, src_buf, dst_buf):
        for k in late:
            start(a2a_one(msg, src_buf, dst_buf, k))

        @pl.when(diag)
        def _():
            dst_buf[z] = src_buf[z]

        @pl.when(jnp.logical_not(diag))
        def _():
            a2a_one(msg, src_buf, dst_buf, 0).start()

    def a2a_wait(msg, src_buf, dst_buf, k):
        came = (z + 8 - k) % NZ

        def wait():
            rcopy(
                src_buf.at[came],
                dst_buf.at[came],
                a2a_s.at[msg, k],
                a2a_r.at[msg, k],
                hpeer(k),
            ).wait_recv()

        if k == 0:
            pl.when(jnp.logical_not(diag))(wait)
        else:
            wait()
        return came

    order = (0, 1, 7, 2, 6, 3, 5, 4)

    def a2a_wait_all(msg, src_buf, dst_buf):
        for k in order:
            a2a_wait(msg, src_buf, dst_buf, k)

    def skv_copy(zb, k):
        return rcopy(kv_buf.at[0, zb], kv_buf.at[1, zb], skv_s.at[k], skv_r.at[k], sibling)

    def forward_kv():
        for k in order:
            zb = a2a_wait(M_KV, kv_send, kv_buf.at[0], k)
            start(skv_copy(zb, k))

    def ones_kv(half):
        def step(b, carry):
            kv1_buf[half, b] = jnp.where(m128, 1.0, kv_buf[half, b].astype(F32)).astype(BF)
            return carry

        lax.fori_loop(0, 8, step, 0)

    def unpack_q():
        def step(b, carry):
            p = q_buf[b].astype(F32)
            zero = jnp.zeros_like(p)
            full = jnp.concatenate([jnp.where(m64, p, zero), jnp.where(m64, swap(p), zero)], 0)
            qz[pl.ds(pl.multiple_of(b * 128, 128), 128), :] = full.astype(BF)
            return carry

        lax.fori_loop(0, 8, step, 0)

    def unpack_g():
        def step(b, carry):
            p = g_buf[b].astype(F32)
            zero = jnp.zeros_like(p)
            full = jnp.concatenate([jnp.where(m64, zero, swap(p)), jnp.where(m64, zero, p)], 0)
            rows = pl.ds(pl.multiple_of(b * 128, 128), 128)
            gz[rows, :] = full.astype(BF)
            both = full + qz[rows, :].astype(F32)
            qgt[b] = both.T.astype(BF)
            return carry

        lax.fori_loop(0, 8, step, 0)

    RB = 256

    def forward(half, first):
        def step(i, carry):
            row = pl.multiple_of(i * RB, RB)
            rows = pl.ds(row, RB)
            q = qz[rows, :]
            total = None
            for t in range(2):
                keys = kv_buf[half, pl.ds(4 * t, 4)].reshape(512, 128)
                s = dot_nt(q, keys)
                w = jnp.exp2(s * (0.125 * LOG2E))
                wexp[half, rows, pl.ds(512 * t, 512)] = w
                vals = kv1_buf[half, pl.ds(4 * t, 4)].reshape(512, 128)
                part = dot(w.astype(BF), vals)
                total = part if total is None else total + part
            if first:
                oacc[rows, :] = total
            else:
                oacc[rows, :] += total
            return carry

        lax.fori_loop(0, 1024 // RB, step, 0)

    def finish_forward():
        def step(b, carry):
            rows = pl.ds(pl.multiple_of(b * 128, 128), 128)
            o = oacc[rows, :]
            sw = swap(o)
            att = rnd(jnp.where(m128, 0.0, o / jnp.where(m128, 1.0, sw)))
            tot = jnp.where(m128, o, sw)
            inv_buf[rows, :] = 1.0 / tot
            att_send[b] = jnp.where(m64, swap(att[:64]), att[64:]).astype(BF)
            oacc[rows, :] = att
            return carry

        lax.fori_loop(0, 8, step, 0)

    def make_delta():
        def step(b, carry):
            rows = pl.ds(pl.multiple_of(b * 128, 128), 128)
            d = jnp.sum(oacc[rows, :] * gz[rows, :].astype(F32), axis=-1, keepdims=True)
            del_buf[rows, :] = jnp.broadcast_to(d, (128, 128))
            return carry

        lax.fori_loop(0, 8, step, 0)

    def backward(half, first):
        dkvt[...] = jnp.zeros_like(dkvt)

        def step(i, carry):
            rows = pl.ds(pl.multiple_of(i * RB, RB), RB)
            g = gz[rows, :]
            inv = inv_buf[rows, 0:1]
            delta = del_buf[rows, 0:1]
            qt = jnp.concatenate([qgt[2 * i], qgt[2 * i + 1]], axis=1)
            total = None
            for t in range(2):
                cols = pl.ds(512 * t, 512)
                keys = kv_buf[half, pl.ds(4 * t, 4)].reshape(512, 128)
                dp = dot_nt(g, keys)
                p = wexp[half, rows, cols] * inv
                ds = (p * (dp - delta)).astype(BF)
                pb = p.astype(BF)
                part = dot(ds, keys)
                total = part if total is None else total + part
                dkvt[0:64, cols] += dot(qt[0:64], ds)
                dkvt[64:128, cols] += dot(qt[64:128], pb)
            if first:
                dq_acc[rows, :] = total
            else:
                dq_acc[rows, :] += total
            return carry

        lax.fori_loop(0, 1024 // RB, step, 0)

    def key_grads(b):
        x = dkvt[:, pl.ds(b * 128, 128)].T
        return x * jnp.where(m128, 0.125, 1.0)

    def sdk_copy(b):
        return rcopy(dkv_x.at[b], dkv_sib.at[b], sdk_s.at[b], sdk_r.at[b], sibling)

    make_normed()
    stage_partner(KV)
    make_noise(0)
    stage_ring(KV, 1, 0)
    make_noise(1)
    stage_ring(KV, 1, 1)
    make_noise(2)
    stage_ring(KV, 2, 0)
    make_noise(3)
    stage_ring(KV, 2, 1)
    stage_own(Q)
    make_noise(4)
    stage_ring(KV, 3, 0)
    stage_partner(Q)
    make_noise(5)
    stage_ring(KV, 3, 1)
    make_noise(6)
    stage_last(KV)
    make_noise(7)
    stage_ring(Q, 1, 0)
    stage_ring(Q, 1, 1)
    stage_sibling(KV)
    form_weight(HD, 2 * HD)
    stage_ring(Q, 2, 0)
    stage_ring(Q, 2, 1)
    stage_own(O)
    project_kv()
    a2a_start(M_KV, kv_send, kv_buf.at[0])
    stage_ring(Q, 3, 0)
    stage_ring(Q, 3, 1)
    stage_partner(O)
    make_u(0)
    stage_last(Q)
    stage_ring(O, 1, 0)
    stage_ring(O, 1, 1)
    stage_sibling(Q)
    form_weight(0, HD)
    project_q()
    a2a_start(M_Q, q_send, q_buf)
    stage_ring(O, 2, 0)
    stage_ring(O, 2, 1)
    forward_kv()
    stage_ring(O, 3, 0)
    stage_ring(O, 3, 1)
    make_u(1)
    ones_kv(0)
    stage_last(O)
    a2a_wait_all(M_Q, q_send, q_buf)
    unpack_q()
    stage_sibling(O)
    project_g()
    a2a_start(M_G, g_send, g_buf)
    forward(0, True)
    for k in order:
        skv_copy((z + 8 - k) % NZ, k).wait_recv()
    ones_kv(1)
    forward(1, False)
    finish_forward()
    a2a_start(M_ATT, att_send, att_buf)
    a2a_wait_all(M_G, g_send, g_buf)
    unpack_g()
    make_delta()
    backward(1, True)
    for b in range(8):
        dkv_x[b] = key_grads(b).astype(BF)
        start(sdk_copy(b))
    backward(0, False)

    def pack_dq(b, carry):
        x = dq_acc[pl.ds(pl.multiple_of(b * 128, 128), 128), :] * 0.125
        dq_send[b] = jnp.where(m64, x[:64], swap(x[64:])).astype(BF)
        return carry

    lax.fori_loop(0, 8, pack_dq, 0)
    a2a_start(M_DQ, dq_send, dq_buf)
    for b in range(8):
        sdk_copy(b).wait_recv()
        dkv_send[b] = (key_grads(b) + dkv_sib[b].astype(F32)).astype(BF)
    a2a_start(M_DKV, dkv_send, dkv_buf)
    make_u(2)

    def join_pair(a, b):
        a, b = a.astype(F32), b.astype(F32)
        return jnp.concatenate([jnp.where(m64, a, swap(b)), jnp.where(m64, swap(a), b)], 0)

    a2a_wait_all(M_ATT, att_send, att_buf)
    att_all = jnp.concatenate(
        [join_pair(att_buf[h], att_buf[h + 1]).astype(BF) for h in range(0, 8, 2)], axis=1
    )
    for t in range(2):
        w = out_buf[:, :, pl.ds(512 * t, 512)].reshape(HD, 512)
        att_out[:, pl.ds(512 * t, 512)] = dot(att_all, w).astype(BF)

    a2a_wait_all(M_DQ, dq_send, dq_buf)
    grads = [join_pair(dq_buf[h], dq_buf[h + 1]) for h in range(0, 8, 2)]
    a2a_wait_all(M_DKV, dkv_send, dkv_buf)
    dks, dvs = [], []
    for h in range(0, 8, 2):
        a, b = dkv_buf[h].astype(F32), dkv_buf[h + 1].astype(F32)
        dks.append(jnp.where(m128, a, swap(b)))
        dvs.append(jnp.where(m128, swap(a), b))
    gproj = jnp.concatenate(grads + dks + dvs, axis=1)

    ps_buf[0, 0] = jnp.sum(gproj * ubuf[...], axis=0, keepdims=True)
    gproj = gproj.astype(BF)

    def ps_copy(stage, k):
        to = (zpeer, ypeer, xgroup)[stage](k)
        return rcopy(
            ps_buf.at[stage, 0], ps_buf.at[stage, k], ps_s.at[stage, k], ps_r.at[stage, k], to
        )

    def ps_start(stage):
        for k in late:
            start(ps_copy(stage, k))

    def ps_sum(stage):
        for k in order[1:]:
            ps_copy(stage, k).wait_recv()
        place = (z, y, xl * 4 + xh * 2 + c)[stage]
        total = None
        for j in range(8):
            v = ps_buf[stage, (place + 8 - j) % 8]
            total = v if total is None else total + v
        return total

    ps_start(0)
    grad = [dot_nt(gproj, wbuf[pl.ds(512 * t, 512), :]) for t in range(2)]
    grad = jnp.concatenate(grad, axis=1)
    ps_buf[1, 0] = ps_sum(0)
    ps_start(1)
    a = anch[...]
    r = lax.rsqrt(jnp.mean(a * a, axis=-1, keepdims=True) + 1e-06)
    d = grad * gain_ref[...]
    ga = r * (d - a * (r * r * jnp.mean(d * a, axis=-1, keepdims=True)))
    hi = ga.astype(BF)
    lo = (ga - hi.astype(F32)).astype(BF)
    ps_buf[2, 0] = ps_sum(1)
    ps_start(2)
    sel_t = (lax.broadcasted_iota(jnp.int32, (PTS, TOK), 0) == idx_ref[...]).astype(BF)
    sel2 = jnp.concatenate([sel_t, sel_t], axis=1)
    for t in range(2):
        cols = slice(512 * t, 512 * t + 512)
        gp_out[:, cols] = dot(sel2, jnp.concatenate([hi[:, cols], lo[:, cols]], axis=0))
    gs_out[...] = ps_sum(2)

    for copy in sends:
        copy.wait_send()

    @pl.when(jnp.logical_not(diag))
    def _():
        for msg, src, dst in (
            (M_KV, kv_send, kv_buf.at[0]),
            (M_Q, q_send, q_buf),
            (M_G, g_send, g_buf),
            (M_ATT, att_send, att_buf),
            (M_DQ, dq_send, dq_buf),
            (M_DKV, dkv_send, dkv_buf),
        ):
            a2a_one(msg, src, dst, 0).wait_send()


def local(points, anchor_index, norm_gain, weight_mean, weight_scale, noise_seed, out_weight, cotangent):
    vm = pl.BlockSpec(memory_space=pltpu.VMEM)
    hbm = pl.BlockSpec(memory_space=pl.ANY)
    V = pltpu.VMEM
    dma = pltpu.SemaphoreType.DMA
    att, gpts, gs = pl.pallas_call(
        body,
        out_shape=(
            jax.ShapeDtypeStruct((TOK, D), BF),
            jax.ShapeDtypeStruct((PTS, D), F32),
            jax.ShapeDtypeStruct((1, 3 * HD), F32),
        ),
        in_specs=[hbm, vm, vm, vm, vm, vm, vm, hbm],
        out_specs=(vm, vm, vm),
        scratch_shapes=[
            V((PTS, D), BF),
            V((TOK, D), BF),
            V((32, 32, 3 * HD), BF),
            V((32, 16, D), BF),
            V((D, 3 * HD), F32),
            V((D, 3 * HD), BF),
            V((D, 3 * HD), BF),
            V((D, 3 * HD), BF),
            V((TOK, D), F32),
            V((TOK, D), BF),
            V((TOK, 3 * HD), F32),
            V((8, 128, 128), BF),
            V((8, 64, 128), BF),
            V((8, 64, 128), BF),
            V((2, 8, 128, 128), BF),
            V((2, 8, 128, 128), BF),
            V((8, 64, 128), BF),
            V((8, 64, 128), BF),
            V((1024, 128), BF),
            V((1024, 128), BF),
            V((8, 128, 128), BF),
            V((2, 1024, 1024), F32),
            V((1024, 128), F32),
            V((1024, 128), F32),
            V((1024, 128), F32),
            V((1024, 128), F32),
            V((128, 1024), F32),
            V((8, 128), F32),
            V((8, 128, 128), BF),
            V((8, 128, 128), BF),
            V((8, 128, 128), BF),
            V((8, 64, 128), BF),
            V((8, 64, 128), BF),
            V((8, 64, 128), BF),
            V((8, 64, 128), BF),
            V((8, 128, 128), BF),
            V((3, 8, 1, 3 * HD), F32),
            dma((2,)),
            dma((3, 2, 4, 2)),
            dma((3, 2, 4, 2)),
            dma((3,)),
            dma((3,)),
            dma((3, 8, 2)),
            dma((3, 8, 2)),
            dma((6, 8)),
            dma((6, 8)),
            dma((8,)),
            dma((8,)),
            dma((8,)),
            dma((8,)),
            dma((3, 8)),
            dma((3, 8)),
        ],
        compiler_params=pltpu.CompilerParams(
            collective_id=0, has_side_effects=True, vmem_limit_bytes=56 * 1024 * 1024
        ),
    )(
        points[0],
        anchor_index,
        norm_gain.reshape(1, D),
        weight_mean,
        weight_scale.reshape(1, 3 * HD),
        noise_seed.reshape(1, 3 * HD),
        out_weight,
        cotangent[0],
    )
    return att[None], gpts[None], gs.reshape(3 * HD)


def solution(mesh):
    in_specs = (
        P("outer", "inner", None),
        P("outer", "inner"),
        P(),
        P("outer", None),
        P(),
        P(),
        P("outer", None),
        P("outer", "inner", None),
    )
    out_specs = (P("outer", "inner", None), P("outer", "inner", None), P())
    return jax.shard_map(local, mesh=mesh, in_specs=in_specs, out_specs=out_specs, check_vma=False)
```

```python
import functools

import jax
import jax.numpy as jnp
from jax import lax
from jax.experimental import pallas as pl
from jax.experimental.pallas import tpu as pltpu
from jax.sharding import PartitionSpec as P

MESH = pl.DeviceIdType.MESH
BF = jnp.bfloat16
F32 = jnp.float32

HEADS = 8
TOK = 128
PTS = 256
D = 1024
HD = 512
NZ = 8
NY = 8
LOG2E = 1.4426950408889634

K, V, Q, O = 0, 1, 2, 3
M_KV, M_Q, M_G, M_UKV, M_UQ, M_ATT, M_DQ, M_DKV = range(8)
AWAY = (4, 3, 5, 0, 2, 6, 1, 7)


def left_half(rows):
    return lax.broadcasted_iota(jnp.int32, (rows, 128), 1) < 64


def swap(x):
    return pltpu.roll(x, 64, 1)


def dot(a, b):
    return jnp.dot(a, b, preferred_element_type=F32)


def dot_nt(a, b):
    return lax.dot_general(a, b, (((1,), (1,)), ((), ())), preferred_element_type=F32)


def body(
    points_hbm,
    idx_hbm,
    gain_hbm,
    mean_hbm,
    scale_hbm,
    seed_hbm,
    outw_hbm,
    cot_hbm,
    att_out,
    hi_out,
    lo_out,
    gs_out,
    idx_out,
    pts,
    cot,
    idx_ref,
    gain_ref,
    mean_ref,
    scale_ref,
    seed_ref,
    outw_ref,
    pbuf,
    obuf,
    ow,
    noise_buf,
    nhi,
    wbuf,
    anch,
    normed,
    kproj,
    kv_send,
    q_send,
    g_send,
    ukv_send,
    uq_send,
    kv_buf,
    kv1_buf,
    q_buf,
    g_buf,
    ukv_buf,
    uq_buf,
    qz,
    gz,
    qgt,
    wexp,
    oacc,
    inv_buf,
    del_buf,
    dq_acc,
    dkvt,
    dkv_x,
    dkv_sib,
    dkv_send,
    att_send,
    dq_send,
    att_buf,
    dq_buf,
    dkv_buf,
    ps_buf,
    loc_sem,
    far_s,
    far_r,
    xo_s,
    xo_r,
    near_s,
    near_r,
    sib_s,
    sib_r,
    a2a_s,
    a2a_r,
    skv_s,
    skv_r,
    sdk_s,
    sdk_r,
    ps_s,
    ps_r,
):
    inner = lax.axis_index("inner")
    outer = lax.axis_index("outer")
    z = inner // 2
    xl = inner % 2
    y = outer // 4
    xh = (outer // 2) % 2
    c = outer % 2

    def dev(z_, xl_, y_, xh_, c_):
        return {"inner": z_ * 2 + xl_, "outer": (y_ * 2 + xh_) * 2 + c_}

    def xgroup(k):
        g = (xl * 4 + xh * 2 + c + k) % 8
        return dev(z, g // 4, y, (g // 2) % 2, g % 2)

    def zpeer(k):
        return dev((z + k) % NZ, xl, y, xh, c)

    def ypeer(k):
        return dev(z, xl, (y + k) % NY, xh, c)

    def rcopy(src, dst, ssem, rsem, to):
        return pltpu.make_async_remote_copy(
            src_ref=src,
            dst_ref=dst,
            send_sem=ssem,
            recv_sem=rsem,
            device_id=to,
            device_id_type=MESH,
        )

    sends = []

    def start(copy):
        copy.start()
        sends.append(copy)

    loads = [
        pltpu.make_async_copy(a, b, loc_sem.at[n])
        for n, (a, b) in enumerate(
            (
                (mean_hbm, mean_ref),
                (outw_hbm, outw_ref),
                (points_hbm, pts),
                (idx_hbm, idx_ref),
                (gain_hbm, gain_ref),
                (seed_hbm, seed_ref),
                (scale_hbm, scale_ref),
                (cot_hbm, cot),
            )
        )
    ]
    for load in loads:
        load.start()

    diag = xl == c
    bar = pltpu.get_barrier_semaphore()

    def hpeer(k):
        return dev((z + k) % NZ, c, y, xh, xl)

    for k in range(1, 8):
        for to in (ypeer(k), xgroup(k), hpeer(k)):
            pl.semaphore_signal(bar, inc=1, device_id=to, device_id_type=MESH)

    @pl.when(jnp.logical_not(diag))
    def _():
        for k in (1, 7):
            pl.semaphore_signal(bar, inc=1, device_id=zpeer(k), device_id_type=MESH)

    colour = (z + 2 * ((xl + xh) % 2)) % 4
    sibling = dev(z, xl, y, xh, 1 - c)
    across = dev(z, 1 - xl, y, 1 - xh, c)
    near = (zpeer(1), zpeer(7), dev(z, 1 - xl, y, xh, c))
    near_add = (3, 1, 2)

    def piece(part, k, core):
        if part == O:
            return obuf.at[k, core]
        return pbuf.at[part, k, core]

    def own_piece():
        loads[0].wait()
        loads[1].wait()
        for part, base in ((K, HD), (V, 2 * HD), (Q, 0)):
            cols = pl.ds(pl.multiple_of(base + colour * 128, 128), 128)
            pbuf[part, colour, c, xh, y] = mean_ref[:, cols]
        cols = pl.ds(pl.multiple_of(colour * 256, 128), 256)
        obuf[colour, c, xh, y] = outw_ref[:, cols]

    def far_copy(part, k, at):
        b = piece(part, colour, c).at[xh, at]
        return rcopy(b, b, far_s.at[part, k], far_r.at[part, k], ypeer(k))

    def gather_far(part):
        for k in (4, 3, 5, 2, 6, 1, 7):
            start(far_copy(part, k, y))

    def half_out(part, r):
        b = piece(part, colour, c).at[(xh + r) % 2]
        for n, to in enumerate(near):
            start(rcopy(b, b, near_s.at[part, r, n], near_r.at[part, r, n], to))
        start(rcopy(b, b, sib_s.at[part, r], sib_r.at[part, r], sibling))

    def gather_mid(part):
        for k in (1, 7, 2, 6, 3, 5, 4):
            far_copy(part, k, (y + 8 - k) % NY).wait_recv()
        b = piece(part, colour, c).at[xh]
        start(rcopy(b, b, xo_s.at[part], xo_r.at[part], across))
        half_out(part, 0)

    def gather_near(part):
        b = piece(part, colour, c).at[1 - xh]
        rcopy(b, b, xo_s.at[part], xo_r.at[part], across).wait_recv()
        half_out(part, 1)

    def sib_copy(part, n, core):
        b = piece(part, (colour + near_add[n]) % 4, core)
        return rcopy(b, b, sib_s.at[part, 2 + n], sib_r.at[part, 2 + n], sibling)

    def gather_sibling(part):
        for n in range(3):
            for r in range(2):
                b = piece(part, (colour + near_add[n]) % 4, c).at[(xh + r) % 2]
                rcopy(b, b, near_s.at[part, r, n], near_r.at[part, r, n], near[n]).wait_recv()
            start(sib_copy(part, n, c))

    def gather_last(part):
        for r in range(2):
            b = piece(part, colour, 1 - c).at[(xh + r) % 2]
            rcopy(b, b, sib_s.at[part, r], sib_r.at[part, r], sibling).wait_recv()
        for n in range(3):
            sib_copy(part, n, 1 - c).wait_recv()

    def make_normed():
        for load in loads[2:5]:
            load.wait()
        sel_t = (
            lax.broadcasted_iota(jnp.int32, (PTS, TOK), 0) == idx_ref[...]
        ).astype(F32)
        a = dot(sel_t.T.astype(BF), pts[...])
        anch[...] = a
        r = lax.rsqrt(jnp.mean(a * a, axis=-1, keepdims=True) + 1e-06)
        normed[...] = (a * r * gain_ref[...]).astype(BF)

    def row_of(ref, col):
        r0 = col // 128
        return jnp.concatenate([ref[r : r + 1, :] for r in range(r0, r0 + 4)], axis=1)

    def make_noise(chunk):
        def step(t, carry):
            row = pl.multiple_of(chunk * 128 + t * 16, 16)
            for col in range(0, 3 * HD, HD):
                cols = pl.ds(col, HD)
                ids = lax.broadcasted_iota(jnp.int32, (16, HD), 0) + row
                h = row_of(seed_ref, col) * 747796405 + 12345 + ids * 1103515245
                h = h ^ lax.shift_right_logical(h, jnp.full_like(h, 15))
                h = h * 277803737
                h = h ^ lax.shift_right_logical(h, jnp.full_like(h, 16))
                h = lax.shift_right_logical(h, jnp.full_like(h, 8)) & 65535
                n = (h.astype(F32) - 32767.5) * (3.4641016 / 65536.0)
                noise_buf[pl.ds(row, 16), cols] = n
                nhi[pl.ds(row, 16), cols] = n.astype(BF)
            return carry

        lax.fori_loop(0, 8, step, 0)

    def rnd(x):
        return x.astype(BF).astype(F32)

    m128 = left_half(128)
    m64 = left_half(64)

    def form_weight(part):
        col = {K: HD, V: 2 * HD, Q: 0}[part]

        def step(s_, carry):
            scale = row_of(scale_ref, col)
            for half, core in ((0, 0), (0, 1), (1, 0), (1, 1)):
                row = pl.multiple_of(s_ * 128 + half * 64 + core * 32, 32)
                for k in range(4):
                    cols = pl.ds(col + 128 * k, 128)
                    w = pbuf[part, k, core, half, s_].astype(F32) + scale[:, 128 * k : 128 * k + 128] * noise_buf[pl.ds(row, 32), cols]
                    wbuf[pl.ds(row, 32), cols] = w.astype(BF)
            return carry

        lax.fori_loop(0, 8, step, 0)

    def form_out():
        def step(s_, carry):
            for half, core in ((0, 0), (0, 1), (1, 0), (1, 1)):
                row = pl.multiple_of(s_ * 64 + half * 32 + core * 16, 16)
                for k in range(4):
                    ow[pl.ds(row, 16), pl.ds(256 * k, 256)] = obuf[k, core, half, s_]
            return carry

        lax.fori_loop(0, 8, step, 0)

    def pack_kv(k2, v2, h0, ref):
        for u in range(2):
            k = k2[:, u * 128 : u * 128 + 128]
            v = v2[:, u * 128 : u * 128 + 128]
            h = h0 + 2 * u
            ref[h] = jnp.where(m128, k, swap(v)).astype(BF)
            ref[h + 1] = jnp.where(m128, swap(k), v).astype(BF)

    def project_k():
        x = normed[...]
        for t in range(2):
            kproj[:, pl.ds(256 * t, 256)] = rnd(dot(x, wbuf[:, pl.ds(HD + 256 * t, 256)]))

    def project_v():
        x = normed[...]
        for t in range(2):
            v2 = rnd(dot(x, wbuf[:, pl.ds(2 * HD + 256 * t, 256)]))
            pack_kv(kproj[:, pl.ds(256 * t, 256)], v2, 4 * t, kv_send)

    def pack_pair(x, h, ref):
        top, bot = x[:64], x[64:]
        ref[h] = jnp.where(m64, top, swap(bot)).astype(BF)
        ref[h + 1] = jnp.where(m64, swap(top), bot).astype(BF)

    def pack_quad(x, t, ref):
        for u in range(2):
            pack_pair(x[:, u * 128 : u * 128 + 128], 4 * t + 2 * u, ref)

    def project_q():
        x = normed[...]
        for t in range(2):
            pack_quad(rnd(dot(x, wbuf[:, pl.ds(256 * t, 256)])), t, q_send)

    def make_ukv():
        x = normed[...]
        for t in range(2):
            k2 = dot(x, nhi[:, pl.ds(HD + 256 * t, 256)])
            v2 = dot(x, nhi[:, pl.ds(2 * HD + 256 * t, 256)])
            pack_kv(k2, v2, 4 * t, ukv_send)

    def make_uq():
        x = normed[...]
        for t in range(2):
            pack_quad(dot(x, nhi[:, pl.ds(256 * t, 256)]), t, uq_send)

    def project_g():
        loads[7].wait()
        x = cot[...]
        for t in range(2):
            pack_quad(rnd(dot_nt(x, ow[pl.ds(256 * t, 256), :])), t, g_send)

    def a2a_one(msg, src_buf, dst_buf, p, back):
        k = AWAY[p]
        if back:
            src, dst, to = src_buf.at[p], dst_buf.at[z], hpeer(8 - k)
        else:
            src, dst, to = src_buf.at[(z + k) % NZ], dst_buf.at[p], hpeer(k)
        return rcopy(src, dst, a2a_s.at[msg, p], a2a_r.at[msg, p], to)

    def a2a_start(msg, src_buf, dst_buf, back=False, slots=range(8)):
        for p in slots:
            if AWAY[p]:
                start(a2a_one(msg, src_buf, dst_buf, p, back))
                continue

            @pl.when(diag)
            def _():
                if back:
                    dst_buf[z] = src_buf[p]
                else:
                    dst_buf[p] = src_buf[z]

            @pl.when(jnp.logical_not(diag))
            def _():
                a2a_one(msg, src_buf, dst_buf, p, back).start()

    def a2a_wait(msg, src_buf, dst_buf, p, back=False):
        k = AWAY[p]

        def wait():
            dst = dst_buf.at[(z + k) % NZ] if back else dst_buf.at[p]
            src = src_buf.at[0]
            rcopy(src, dst, a2a_s.at[msg, p], a2a_r.at[msg, p], hpeer(k)).wait_recv()

        if k == 0:
            pl.when(jnp.logical_not(diag))(wait)
        else:
            wait()

    order = (3, 6, 7, 4, 5, 1, 2, 0)

    def a2a_wait_all(msg, src_buf, dst_buf, back=False):
        for p in order:
            a2a_wait(msg, src_buf, dst_buf, p, back)

    def skv_copy(p):
        return rcopy(kv_buf.at[0, p], kv_buf.at[1, p], skv_s.at[p], skv_r.at[p], sibling)

    def forward_kv():
        for p in order:
            a2a_wait(M_KV, kv_send, kv_buf.at[0], p)
            start(skv_copy(p))

    def ones_kv(half):
        def step(b, carry):
            kv1_buf[half, b] = jnp.where(m128, 1.0, kv_buf[half, b].astype(F32)).astype(BF)
            return carry

        lax.fori_loop(0, 8, step, 0)

    def unpack_q():
        def step(b, carry):
            p = q_buf[b].astype(F32)
            zero = jnp.zeros_like(p)
            full = jnp.concatenate([jnp.where(m64, p, zero), jnp.where(m64, swap(p), zero)], 0)
            qz[pl.ds(pl.multiple_of(b * 128, 128), 128), :] = full.astype(BF)
            return carry

        lax.fori_loop(0, 8, step, 0)

    def unpack_g():
        def step(b, carry):
            p = g_buf[b].astype(F32)
            zero = jnp.zeros_like(p)
            full = jnp.concatenate([jnp.where(m64, zero, swap(p)), jnp.where(m64, zero, p)], 0)
            rows = pl.ds(pl.multiple_of(b * 128, 128), 128)
            gz[rows, :] = full.astype(BF)
            both = full + qz[rows, :].astype(F32)
            qgt[b] = both.T.astype(BF)
            return carry

        lax.fori_loop(0, 8, step, 0)

    RB = 256

    def forward(half, first):
        def step(i, carry):
            row = pl.multiple_of(i * RB, RB)
            rows = pl.ds(row, RB)
            q = qz[rows, :]
            total = None
            for t in range(2):
                keys = kv_buf[half, pl.ds(4 * t, 4)].reshape(512, 128)
                s = dot_nt(q, keys)
                w = jnp.exp2(s * (0.125 * LOG2E))
                wexp[half, rows, pl.ds(512 * t, 512)] = w
                vals = kv1_buf[half, pl.ds(4 * t, 4)].reshape(512, 128)
                part = dot(w.astype(BF), vals)
                total = part if total is None else total + part
            if first:
                oacc[rows, :] = total
            else:
                oacc[rows, :] += total
            return carry

        lax.fori_loop(0, 1024 // RB, step, 0)

    def finish_forward():
        def step(b, carry):
            rows = pl.ds(pl.multiple_of(b * 128, 128), 128)
            o = oacc[rows, :]
            sw = swap(o)
            att = rnd(jnp.where(m128, 0.0, o / jnp.where(m128, 1.0, sw)))
            tot = jnp.where(m128, o, sw)
            inv_buf[rows, :] = 1.0 / tot
            att_send[b] = jnp.where(m64, swap(att[:64]), att[64:]).astype(BF)
            oacc[rows, :] = att
            return carry

        lax.fori_loop(0, 8, step, 0)

    def make_delta():
        def step(b, carry):
            rows = pl.ds(pl.multiple_of(b * 128, 128), 128)
            d = jnp.sum(oacc[rows, :] * gz[rows, :].astype(F32), axis=-1, keepdims=True)
            del_buf[rows, :] = jnp.broadcast_to(d, (128, 128))
            return carry

        lax.fori_loop(0, 8, step, 0)

    def backward(half, t, first):
        cols = pl.ds(512 * t, 512)
        dkvt[...] = jnp.zeros_like(dkvt)

        def step(i, carry):
            rows = pl.ds(pl.multiple_of(i * RB, RB), RB)
            qt = jnp.concatenate([qgt[2 * i], qgt[2 * i + 1]], axis=1)
            keys = kv_buf[half, pl.ds(4 * t, 4)].reshape(512, 128)
            dp = dot_nt(gz[rows, :], keys)
            p = wexp[half, rows, cols] * inv_buf[rows, 0:1]
            ds = (p * (dp - del_buf[rows, 0:1])).astype(BF)
            part = dot(ds, keys)
            dkvt[0:64, :] += dot(qt[0:64], ds)
            dkvt[64:128, :] += dot(qt[64:128], p.astype(BF))
            if first:
                dq_acc[rows, :] = part
            else:
                dq_acc[rows, :] += part
            return carry

        lax.fori_loop(0, 1024 // RB, step, 0)

    def key_grads(u):
        x = dkvt[:, u * 128 : u * 128 + 128].T
        return x * jnp.where(m128, 0.125, 1.0)

    def sdk_copy(p):
        return rcopy(dkv_x.at[p], dkv_sib.at[p], sdk_s.at[p], sdk_r.at[p], sibling)

    own_piece()
    @pl.when(diag)
    def _():
        pl.semaphore_wait(bar, 21)

    @pl.when(jnp.logical_not(diag))
    def _():
        pl.semaphore_wait(bar, 23)

    gather_far(K)
    gather_far(V)
    make_normed()
    loads[5].wait()
    loads[6].wait()
    for chunk in range(8):
        make_noise(chunk)
    gather_mid(K)
    gather_far(Q)
    make_uq()
    a2a_start(M_UQ, uq_send, uq_buf)
    gather_mid(V)
    gather_near(K)
    gather_far(O)
    make_ukv()
    gather_near(V)
    gather_sibling(K)
    gather_mid(Q)
    gather_last(K)
    form_weight(K)
    project_k()
    gather_near(Q)
    gather_sibling(V)
    gather_mid(O)
    gather_last(V)
    form_weight(V)
    project_v()
    a2a_start(M_KV, kv_send, kv_buf.at[0])
    gather_near(O)
    gather_sibling(Q)
    gather_last(Q)
    form_weight(Q)
    project_q()
    a2a_start(M_Q, q_send, q_buf)
    gather_sibling(O)
    forward_kv()
    gather_last(O)
    form_out()
    project_g()
    a2a_start(M_G, g_send, g_buf)
    ones_kv(0)
    a2a_wait_all(M_Q, q_send, q_buf)
    unpack_q()
    forward(0, True)
    for p in order:
        skv_copy(p).wait_recv()
    ones_kv(1)
    a2a_start(M_UKV, ukv_send, ukv_buf)
    forward(1, False)
    finish_forward()
    a2a_start(M_ATT, att_send, att_buf, True)
    a2a_wait_all(M_G, g_send, g_buf)
    unpack_g()
    make_delta()
    for t in range(2):
        backward(1, t, t == 0)
        for u in range(4):
            dkv_x[4 * t + u] = key_grads(u).astype(BF)
            start(sdk_copy(4 * t + u))
    a2a_wait_all(M_UKV, ukv_send, ukv_buf)
    a2a_wait_all(M_UQ, uq_send, uq_buf)
    scale_kv = None
    for t in range(2):
        backward(0, t, False)
        for p in range(4 * t, 4 * t + 4):
            sdk_copy(p).wait_recv()
            g = (key_grads(p - 4 * t) + dkv_sib[p].astype(F32)).astype(BF)
            dkv_send[p] = g
            g = g.astype(F32) * ukv_buf[p].astype(F32)
            scale_kv = g if scale_kv is None else scale_kv + g
        a2a_start(M_DKV, dkv_send, dkv_buf, True, range(4 * t, 4 * t + 4))
    scale_q = None
    for p in range(8):
        x = dq_acc[pl.ds(p * 128, 128), :] * 0.125
        g = jnp.where(m64, x[:64], swap(x[64:])).astype(BF)
        dq_send[p] = g
        g = g.astype(F32) * uq_buf[p].astype(F32)
        scale_q = g if scale_q is None else scale_q + g
    a2a_start(M_DQ, dq_send, dq_buf, True)
    scale_q = jnp.sum(scale_q, axis=0, keepdims=True)
    scale_q = scale_q + swap(scale_q)
    scale_kv = jnp.sum(scale_kv, axis=0, keepdims=True)
    idx_out[...] = idx_ref[...]
    first_row = lax.broadcasted_iota(jnp.int32, (8, 128), 0) == 0
    ps_buf[0, 0] = jnp.where(first_row, scale_q, scale_kv)

    def ps_copy(stage, k):
        to = (xgroup, ypeer, hpeer)[stage](k)
        return rcopy(ps_buf.at[stage, 0], ps_buf.at[stage, k], ps_s.at[stage, k], ps_r.at[stage, k], to)

    def ps_start(stage):
        for k in (4, 3, 5, 2, 6, 1, 7):
            start(ps_copy(stage, k))

    def ps_wait(stage):
        for k in (1, 7, 2, 6, 3, 5, 4):
            ps_copy(stage, k).wait_recv()

    def ps_sum(stage):
        ps_wait(stage)
        mine = (xl * 4 + xh * 2 + c, y)[stage]
        total = None
        for j in range(8):
            v = ps_buf[stage, (mine + 8 - j) % 8]
            total = v if total is None else total + v
        return total

    ps_start(0)

    def join_pair(a, b):
        a, b = a.astype(F32), b.astype(F32)
        return jnp.concatenate([jnp.where(m64, a, swap(b)), jnp.where(m64, swap(a), b)], 0)

    a2a_wait_all(M_ATT, att_send, att_buf, True)
    att_all = jnp.concatenate(
        [join_pair(att_buf[h], att_buf[h + 1]).astype(BF) for h in range(0, 8, 2)], axis=1
    )
    for t in range(2):
        att_out[:, pl.ds(512 * t, 512)] = dot(att_all, ow[:, pl.ds(512 * t, 512)]).astype(BF)
    ps_buf[1, 0] = ps_sum(0)
    ps_start(1)

    a2a_wait_all(M_DKV, dkv_send, dkv_buf, True)
    dks, dvs = [], []
    for h in range(0, 8, 2):
        a, b = dkv_buf[h].astype(F32), dkv_buf[h + 1].astype(F32)
        dks.append(jnp.where(m128, a, swap(b)))
        dvs.append(jnp.where(m128, swap(a), b))
    gkv = jnp.concatenate(dks + dvs, axis=1).astype(BF)
    grad = [dot_nt(gkv, wbuf[pl.ds(512 * t, 512), HD:]) for t in range(2)]
    ps_buf[2, 0] = ps_sum(1)
    ps_start(2)
    a2a_wait_all(M_DQ, dq_send, dq_buf, True)
    gq = [join_pair(dq_buf[h], dq_buf[h + 1]) for h in range(0, 8, 2)]
    gq = jnp.concatenate(gq, axis=1).astype(BF)
    grad = [grad[t] + dot_nt(gq, wbuf[pl.ds(512 * t, 512), :HD]) for t in range(2)]
    grad = jnp.concatenate(grad, axis=1)
    a = anch[...]
    r = lax.rsqrt(jnp.mean(a * a, axis=-1, keepdims=True) + 1e-06)
    d = grad * gain_ref[...]
    ga = r * (d - a * (r * r * jnp.mean(d * a, axis=-1, keepdims=True)))
    hi = ga.astype(BF)
    hi_out[...] = hi
    lo_out[...] = (ga - hi.astype(F32)).astype(BF)
    ps_wait(2)
    m8 = left_half(8)
    for j in range(4):
        a, b = (ps_buf[2, (z + 8 - h) % 8] for h in (2 * j, 2 * j + 1))
        qk = jnp.where(m8, a, swap(b))
        gs_out[j : j + 1, :] = qk[0:1]
        gs_out[4 + j : 5 + j, :] = qk[1:2]
        gs_out[8 + j : 9 + j, :] = jnp.where(m8, swap(a), b)[1:2]

    for copy in sends:
        copy.wait_send()

    @pl.when(jnp.logical_not(diag))
    def _():
        for msg, src, dst, back in (
            (M_KV, kv_send, kv_buf.at[0], False),
            (M_Q, q_send, q_buf, False),
            (M_G, g_send, g_buf, False),
            (M_UKV, ukv_send, ukv_buf, False),
            (M_UQ, uq_send, uq_buf, False),
            (M_ATT, att_send, att_buf, True),
            (M_DQ, dq_send, dq_buf, True),
            (M_DKV, dkv_send, dkv_buf, True),
        ):
            a2a_one(msg, src, dst, 3, back).wait_send()


def finish(idx_ref, att_ref, hi_ref, lo_ref, gs_ref, att_out, gp_out, gs_out):
    sel_t = (lax.broadcasted_iota(jnp.int32, (PTS, TOK), 0) == idx_ref[...]).astype(BF)
    sel2 = jnp.concatenate([sel_t, sel_t], axis=1)
    for t in range(2):
        cols = pl.ds(512 * t, 512)
        gp_out[:, cols] = dot(sel2, jnp.concatenate([hi_ref[:, cols], lo_ref[:, cols]], axis=0))
    att_out[...] = att_ref[...]
    gs_out[...] = gs_ref[...]


def local(points, anchor_index, norm_gain, weight_mean, weight_scale, noise_seed, out_weight, cotangent):
    vm = pl.BlockSpec(memory_space=pltpu.VMEM)
    hbm = pl.BlockSpec(memory_space=pltpu.HBM)
    V_ = pltpu.VMEM
    dma = pltpu.SemaphoreType.DMA
    att, hi, lo, gs, idx = pl.pallas_call(
        body,
        out_shape=(
            jax.ShapeDtypeStruct((TOK, D), BF),
            jax.ShapeDtypeStruct((TOK, D), BF),
            jax.ShapeDtypeStruct((TOK, D), BF),
            jax.ShapeDtypeStruct((12, 128), F32),
            jax.ShapeDtypeStruct((1, TOK), jnp.int32),
        ),
        in_specs=[hbm] * 8,
        out_specs=(vm, vm, vm, vm, vm),
        scratch_shapes=[
            V_((PTS, D), BF),
            V_((TOK, D), BF),
            V_((1, TOK), jnp.int32),
            V_((1, D), F32),
            V_((32, 3 * HD), BF),
            V_((12, 128), F32),
            V_((12, 128), jnp.int32),
            V_((16, D), BF),
            V_((3, 4, 2, 2, 8, 32, 128), BF),
            V_((4, 2, 2, 8, 16, 256), BF),
            V_((HD, D), BF),
            V_((D, 3 * HD), F32),
            V_((D, 3 * HD), BF),
            V_((D, 3 * HD), BF),
            V_((TOK, D), F32),
            V_((TOK, D), BF),
            V_((TOK, HD), F32),
            V_((8, 128, 128), BF),
            V_((8, 64, 128), BF),
            V_((8, 64, 128), BF),
            V_((8, 128, 128), BF),
            V_((8, 64, 128), BF),
            V_((2, 8, 128, 128), BF),
            V_((2, 8, 128, 128), BF),
            V_((8, 64, 128), BF),
            V_((8, 64, 128), BF),
            V_((8, 128, 128), BF),
            V_((8, 64, 128), BF),
            V_((1024, 128), BF),
            V_((1024, 128), BF),
            V_((8, 128, 128), BF),
            V_((2, 1024, 1024), F32),
            V_((1024, 128), F32),
            V_((1024, 128), F32),
            V_((1024, 128), F32),
            V_((1024, 128), F32),
            V_((128, 512), F32),
            V_((8, 128, 128), BF),
            V_((8, 128, 128), BF),
            V_((8, 128, 128), BF),
            V_((8, 64, 128), BF),
            V_((8, 64, 128), BF),
            V_((8, 64, 128), BF),
            V_((8, 64, 128), BF),
            V_((8, 128, 128), BF),
            V_((3, 8, 8, 128), F32),
            dma((8,)),
            dma((4, 8)),
            dma((4, 8)),
            dma((4,)),
            dma((4,)),
            dma((4, 2, 3)),
            dma((4, 2, 3)),
            dma((4, 5)),
            dma((4, 5)),
            dma((8, 8)),
            dma((8, 8)),
            dma((8,)),
            dma((8,)),
            dma((8,)),
            dma((8,)),
            dma((3, 8)),
            dma((3, 8)),
        ],
        compiler_params=pltpu.CompilerParams(
            collective_id=0, has_side_effects=True, vmem_limit_bytes=44 * 1024 * 1024
        ),
    )(*(
        pltpu.with_memory_space_constraint(x, pltpu.HBM)
        for x in (
            points[0],
            anchor_index,
            norm_gain.reshape(1, D),
            weight_mean,
            weight_scale.reshape(12, 128),
            noise_seed.reshape(12, 128),
            out_weight,
            cotangent[0],
        )
    ))
    att, gpts, gs = pl.pallas_call(
        finish,
        out_shape=(
            jax.ShapeDtypeStruct((TOK, D), BF),
            jax.ShapeDtypeStruct((PTS, D), F32),
            jax.ShapeDtypeStruct((12, 128), F32),
        ),
        in_specs=[vm] * 5,
        out_specs=(vm, vm, vm),
        compiler_params=pltpu.CompilerParams(vmem_limit_bytes=8 * 1024 * 1024),
    )(idx, att, hi, lo, gs)
    return att[None], gpts[None], gs.reshape(3 * HD)


def solution(mesh):
    in_specs = (
        P("outer", "inner", None),
        P("outer", "inner"),
        P(),
        P("outer", None),
        P(),
        P(),
        P("outer", None),
        P("outer", "inner", None),
    )
    out_specs = (P("outer", "inner", None), P("outer", "inner", None), P())
    return jax.shard_map(local, mesh=mesh, in_specs=in_specs, out_specs=out_specs, check_vma=False)
```

```python
import functools

import jax
import jax.numpy as jnp
from jax import lax
from jax.experimental import pallas as pl
from jax.experimental.pallas import tpu as pltpu
from jax.sharding import PartitionSpec as P

MESH = pl.DeviceIdType.MESH
BF = jnp.bfloat16
F32 = jnp.float32

HEADS = 8
TOK = 128
PTS = 256
D = 1024
HD = 512
NZ = 8
NY = 8
LOG2E = 1.4426950408889634

K, V, Q, O = 0, 1, 2, 3
M_KV, M_Q, M_G, M_UKV, M_UQ, M_ATT, M_DQ, M_DKV = range(8)
AWAY = (4, 3, 5, 0, 2, 6, 1, 7)


def left_half(rows):
    return lax.broadcasted_iota(jnp.int32, (rows, 128), 1) < 64


def swap(x):
    return pltpu.roll(x, 64, 1)


def dot(a, b):
    return jnp.dot(a, b, preferred_element_type=F32)


def dot_nt(a, b):
    return lax.dot_general(a, b, (((1,), (1,)), ((), ())), preferred_element_type=F32)


def body(
    points_hbm,
    idx_hbm,
    gain_hbm,
    mean_hbm,
    scale_hbm,
    seed_hbm,
    outw_hbm,
    cot_hbm,
    att_out,
    hi_out,
    lo_out,
    gs_out,
    idx_out,
    pts,
    cot,
    idx_ref,
    gain_ref,
    mean_ref,
    scale_ref,
    seed_ref,
    outw_ref,
    pbuf,
    obuf,
    ow,
    noise_buf,
    nhi,
    wbuf,
    anch,
    normed,
    kproj,
    kv_send,
    q_send,
    g_send,
    ukv_send,
    uq_send,
    kv_buf,
    kv1_buf,
    q_buf,
    g_buf,
    ukv_buf,
    uq_buf,
    qz,
    gz,
    qgt,
    wexp,
    oacc,
    inv_buf,
    del_buf,
    dq_acc,
    dkvt,
    dkv_x,
    dkv_sib,
    dkv_send,
    att_send,
    dq_send,
    att_buf,
    dq_buf,
    dkv_buf,
    ps_buf,
    loc_sem,
    far_s,
    far_r,
    xo_s,
    xo_r,
    near_s,
    near_r,
    sib_s,
    sib_r,
    a2a_s,
    a2a_r,
    skv_s,
    skv_r,
    sdk_s,
    sdk_r,
    ps_s,
    ps_r,
):
    inner = lax.axis_index("inner")
    outer = lax.axis_index("outer")
    z = inner // 2
    xl = inner % 2
    y = outer // 4
    xh = (outer // 2) % 2
    c = outer % 2

    def dev(z_, xl_, y_, xh_, c_):
        return {"inner": z_ * 2 + xl_, "outer": (y_ * 2 + xh_) * 2 + c_}

    def xgroup(k):
        g = (xl * 4 + xh * 2 + c + k) % 8
        return dev(z, g // 4, y, (g // 2) % 2, g % 2)

    def cross(k):
        return dev(z, 1 - xl, (y + k) % NY, 1 - xh, c)

    def zpeer(k):
        return dev((z + k) % NZ, xl, y, xh, c)

    def ypeer(k):
        return dev(z, xl, (y + k) % NY, xh, c)

    def rcopy(src, dst, ssem, rsem, to):
        return pltpu.make_async_remote_copy(
            src_ref=src,
            dst_ref=dst,
            send_sem=ssem,
            recv_sem=rsem,
            device_id=to,
            device_id_type=MESH,
        )

    sends = []

    def start(copy):
        copy.start()
        sends.append(copy)

    loads = [
        pltpu.make_async_copy(a, b, loc_sem.at[n])
        for n, (a, b) in enumerate(
            (
                (mean_hbm, mean_ref),
                (outw_hbm, outw_ref),
                (points_hbm, pts),
                (idx_hbm, idx_ref),
                (gain_hbm, gain_ref),
                (seed_hbm, seed_ref),
                (scale_hbm, scale_ref),
                (cot_hbm, cot),
            )
        )
    ]
    for load in loads:
        load.start()

    diag = xl == c
    bar = pltpu.get_barrier_semaphore()

    def hpeer(k):
        return dev((z + k) % NZ, c, y, xh, xl)

    for k in range(1, 8):
        for to in (ypeer(k), xgroup(k), hpeer(k)):
            pl.semaphore_signal(bar, inc=1, device_id=to, device_id_type=MESH)

    @pl.when(jnp.logical_not(diag))
    def _():
        for k in (1, 7):
            pl.semaphore_signal(bar, inc=1, device_id=zpeer(k), device_id_type=MESH)

    colour = (z + 2 * ((xl + xh) % 2)) % 4
    sibling = dev(z, xl, y, xh, 1 - c)
    across = dev(z, 1 - xl, y, 1 - xh, c)
    near = (zpeer(1), zpeer(7), dev(z, 1 - xl, y, xh, c))
    near_add = (3, 1, 2)

    def piece(part, k, core):
        if part == O:
            return obuf.at[k, core]
        return pbuf.at[part, k, core]

    def own_piece():
        loads[0].wait()
        loads[1].wait()
        for part, base in ((K, HD), (V, 2 * HD), (Q, 0)):
            cols = pl.ds(pl.multiple_of(base + colour * 128, 128), 128)
            pbuf[part, colour, c, xh, y] = mean_ref[:, cols]
        cols = pl.ds(pl.multiple_of(colour * 256, 128), 256)
        obuf[colour, c, xh, y] = outw_ref[:, cols]

    def far_copy(part, k, at):
        b = piece(part, colour, c).at[xh, at]
        return rcopy(b, b, far_s.at[part, k], far_r.at[part, k], ypeer(k))

    def gather_far(part):
        for k in (4, 3, 5, 2, 6, 1, 7):
            start(far_copy(part, k, y))

    def half_out(part, r):
        b = piece(part, colour, c).at[(xh + r) % 2]
        for n, to in enumerate(near):
            start(rcopy(b, b, near_s.at[part, r, n], near_r.at[part, r, n], to))
        start(rcopy(b, b, sib_s.at[part, r], sib_r.at[part, r], sibling))

    def gather_mid(part):
        for k in (1, 7, 2, 6, 3, 5, 4):
            far_copy(part, k, (y + 8 - k) % NY).wait_recv()
        b = piece(part, colour, c).at[xh]
        start(rcopy(b, b, xo_s.at[part], xo_r.at[part], across))
        half_out(part, 0)

    def gather_near(part):
        b = piece(part, colour, c).at[1 - xh]
        rcopy(b, b, xo_s.at[part], xo_r.at[part], across).wait_recv()
        half_out(part, 1)

    def sib_copy(part, n, core):
        b = piece(part, (colour + near_add[n]) % 4, core)
        return rcopy(b, b, sib_s.at[part, 2 + n], sib_r.at[part, 2 + n], sibling)

    def gather_sibling(part):
        for n in range(3):
            for r in range(2):
                b = piece(part, (colour + near_add[n]) % 4, c).at[(xh + r) % 2]
                rcopy(b, b, near_s.at[part, r, n], near_r.at[part, r, n], near[n]).wait_recv()
            start(sib_copy(part, n, c))

    def gather_last(part):
        for r in range(2):
            b = piece(part, colour, 1 - c).at[(xh + r) % 2]
            rcopy(b, b, sib_s.at[part, r], sib_r.at[part, r], sibling).wait_recv()
        for n in range(3):
            sib_copy(part, n, 1 - c).wait_recv()

    def make_normed():
        for load in loads[2:5]:
            load.wait()
        sel_t = (
            lax.broadcasted_iota(jnp.int32, (PTS, TOK), 0) == idx_ref[...]
        ).astype(F32)
        a = dot(sel_t.T.astype(BF), pts[...])
        anch[...] = a
        r = lax.rsqrt(jnp.mean(a * a, axis=-1, keepdims=True) + 1e-06)
        normed[...] = (a * r * gain_ref[...]).astype(BF)

    def row_of(ref, col):
        r0 = col // 128
        return jnp.concatenate([ref[r : r + 1, :] for r in range(r0, r0 + 4)], axis=1)

    def make_noise(chunk):
        def step(t, carry):
            row = pl.multiple_of(chunk * 128 + t * 16, 16)
            for col in range(0, 3 * HD, HD):
                cols = pl.ds(col, HD)
                ids = lax.broadcasted_iota(jnp.int32, (16, HD), 0) + row
                h = row_of(seed_ref, col) * 747796405 + 12345 + ids * 1103515245
                h = h ^ lax.shift_right_logical(h, jnp.full_like(h, 15))
                h = h * 277803737
                h = h ^ lax.shift_right_logical(h, jnp.full_like(h, 16))
                h = lax.shift_right_logical(h, jnp.full_like(h, 8)) & 65535
                n = (h.astype(F32) - 32767.5) * (3.4641016 / 65536.0)
                noise_buf[pl.ds(row, 16), cols] = n
                nhi[pl.ds(row, 16), cols] = n.astype(BF)
            return carry

        lax.fori_loop(0, 8, step, 0)

    def rnd(x):
        return x.astype(BF).astype(F32)

    m128 = left_half(128)
    m64 = left_half(64)

    def form_weight(part):
        col = {K: HD, V: 2 * HD, Q: 0}[part]

        def step(s_, carry):
            scale = row_of(scale_ref, col)
            for half, core in ((0, 0), (0, 1), (1, 0), (1, 1)):
                row = pl.multiple_of(s_ * 128 + half * 64 + core * 32, 32)
                for k in range(4):
                    cols = pl.ds(col + 128 * k, 128)
                    w = pbuf[part, k, core, half, s_].astype(F32) + scale[:, 128 * k : 128 * k + 128] * noise_buf[pl.ds(row, 32), cols]
                    wbuf[pl.ds(row, 32), cols] = w.astype(BF)
            return carry

        lax.fori_loop(0, 8, step, 0)

    def form_out():
        def step(s_, carry):
            for half, core in ((0, 0), (0, 1), (1, 0), (1, 1)):
                row = pl.multiple_of(s_ * 64 + half * 32 + core * 16, 16)
                for k in range(4):
                    ow[pl.ds(row, 16), pl.ds(256 * k, 256)] = obuf[k, core, half, s_]
            return carry

        lax.fori_loop(0, 8, step, 0)

    def pack_kv(k2, v2, h0, ref):
        for u in range(2):
            k = k2[:, u * 128 : u * 128 + 128]
            v = v2[:, u * 128 : u * 128 + 128]
            h = h0 + 2 * u
            ref[h] = jnp.where(m128, k, swap(v)).astype(BF)
            ref[h + 1] = jnp.where(m128, swap(k), v).astype(BF)

    def project_k():
        x = normed[...]
        for t in range(2):
            kproj[:, pl.ds(256 * t, 256)] = rnd(dot(x, wbuf[:, pl.ds(HD + 256 * t, 256)]))

    def project_v():
        x = normed[...]
        for t in range(2):
            v2 = rnd(dot(x, wbuf[:, pl.ds(2 * HD + 256 * t, 256)]))
            pack_kv(kproj[:, pl.ds(256 * t, 256)], v2, 4 * t, kv_send)

    def pack_pair(x, h, ref):
        top, bot = x[:64], x[64:]
        ref[h] = jnp.where(m64, top, swap(bot)).astype(BF)
        ref[h + 1] = jnp.where(m64, swap(top), bot).astype(BF)

    def pack_quad(x, t, ref):
        for u in range(2):
            pack_pair(x[:, u * 128 : u * 128 + 128], 4 * t + 2 * u, ref)

    def project_q():
        x = normed[...]
        for t in range(2):
            pack_quad(rnd(dot(x, wbuf[:, pl.ds(256 * t, 256)])), t, q_send)

    def make_ukv():
        x = normed[...]
        for t in range(2):
            k2 = dot(x, nhi[:, pl.ds(HD + 256 * t, 256)])
            v2 = dot(x, nhi[:, pl.ds(2 * HD + 256 * t, 256)])
            pack_kv(k2, v2, 4 * t, ukv_send)

    def make_uq():
        x = normed[...]
        for t in range(2):
            pack_quad(dot(x, nhi[:, pl.ds(256 * t, 256)]), t, uq_send)

    def project_g():
        loads[7].wait()
        x = cot[...]
        for t in range(2):
            pack_quad(rnd(dot_nt(x, ow[pl.ds(256 * t, 256), :])), t, g_send)

    def a2a_one(msg, src_buf, dst_buf, p, back):
        k = AWAY[p]
        if back:
            src, dst, to = src_buf.at[p], dst_buf.at[z], hpeer(8 - k)
        else:
            src, dst, to = src_buf.at[(z + k) % NZ], dst_buf.at[p], hpeer(k)
        return rcopy(src, dst, a2a_s.at[msg, p], a2a_r.at[msg, p], to)

    def a2a_start(msg, src_buf, dst_buf, back=False, slots=range(8)):
        for p in slots:
            if AWAY[p]:
                start(a2a_one(msg, src_buf, dst_buf, p, back))
                continue

            @pl.when(diag)
            def _():
                if back:
                    dst_buf[z] = src_buf[p]
                else:
                    dst_buf[p] = src_buf[z]

            @pl.when(jnp.logical_not(diag))
            def _():
                a2a_one(msg, src_buf, dst_buf, p, back).start()

    def a2a_wait(msg, src_buf, dst_buf, p, back=False):
        k = AWAY[p]

        def wait():
            dst = dst_buf.at[(z + k) % NZ] if back else dst_buf.at[p]
            src = src_buf.at[0]
            rcopy(src, dst, a2a_s.at[msg, p], a2a_r.at[msg, p], hpeer(k)).wait_recv()

        if k == 0:
            pl.when(jnp.logical_not(diag))(wait)
        else:
            wait()

    order = (3, 6, 7, 4, 5, 1, 2, 0)

    def a2a_wait_all(msg, src_buf, dst_buf, back=False):
        for p in order:
            a2a_wait(msg, src_buf, dst_buf, p, back)

    def skv_copy(p):
        return rcopy(kv_buf.at[0, p], kv_buf.at[1, p], skv_s.at[p], skv_r.at[p], sibling)

    def forward_kv():
        for p in order:
            a2a_wait(M_KV, kv_send, kv_buf.at[0], p)
            start(skv_copy(p))

    def ones_kv(half):
        def step(b, carry):
            kv1_buf[half, b] = jnp.where(m128, 1.0, kv_buf[half, b].astype(F32)).astype(BF)
            return carry

        lax.fori_loop(0, 8, step, 0, unroll=True)

    def unpack_q(b):
        p = q_buf[b].astype(F32)
        zero = jnp.zeros_like(p)
        full = jnp.concatenate([jnp.where(m64, p, zero), jnp.where(m64, swap(p), zero)], 0)
        qz[pl.ds(b * 128, 128), :] = full.astype(BF)

    def unpack_g():
        def step(b, carry):
            p = g_buf[b].astype(F32)
            zero = jnp.zeros_like(p)
            full = jnp.concatenate([jnp.where(m64, zero, swap(p)), jnp.where(m64, zero, p)], 0)
            rows = pl.ds(pl.multiple_of(b * 128, 128), 128)
            gz[rows, :] = full.astype(BF)
            both = full + qz[rows, :].astype(F32)
            qgt[b] = both.T.astype(BF)
            return carry

        lax.fori_loop(0, 8, step, 0, unroll=True)

    RB = 512

    def forward_rows(half, i, first):
        rows = pl.ds(pl.multiple_of(i * RB, RB), RB)
        q = qz[rows, :]
        total = None
        for t in range(2):
            keys = kv_buf[half, pl.ds(4 * t, 4)].reshape(512, 128)
            s = dot_nt(q, keys)
            w = jnp.exp2(s * (0.125 * LOG2E))
            wexp[half, rows, pl.ds(512 * t, 512)] = w
            vals = kv1_buf[half, pl.ds(4 * t, 4)].reshape(512, 128)
            part = dot(w.astype(BF), vals)
            total = part if total is None else total + part
        if first:
            oacc[rows, :] = total
        else:
            oacc[rows, :] += total

    def forward_first():
        for p in order:
            a2a_wait(M_Q, q_send, q_buf, p)
        for p in range(8):
            unpack_q(p)

        def step(i, carry):
            forward_rows(0, i, True)
            return carry

        lax.fori_loop(0, 1024 // RB, step, 0)

    def forward_second():
        def step(i, carry):
            forward_rows(1, i, False)
            return carry

        lax.fori_loop(0, 1024 // RB, step, 0)

    def finish_forward():
        def step(b, carry):
            rows = pl.ds(pl.multiple_of(b * 128, 128), 128)
            o = oacc[rows, :]
            sw = swap(o)
            att = rnd(jnp.where(m128, 0.0, o / jnp.where(m128, 1.0, sw)))
            tot = jnp.where(m128, o, sw)
            inv_buf[rows, :] = 1.0 / tot
            att_send[b] = jnp.where(m64, swap(att[:64]), att[64:]).astype(BF)
            oacc[rows, :] = att
            return carry

        lax.fori_loop(0, 8, step, 0, unroll=True)

    def make_delta():
        def step(b, carry):
            rows = pl.ds(pl.multiple_of(b * 128, 128), 128)
            d = jnp.sum(oacc[rows, :] * gz[rows, :].astype(F32), axis=-1, keepdims=True)
            del_buf[rows, :] = jnp.broadcast_to(d, (128, 128))
            return carry

        lax.fori_loop(0, 8, step, 0, unroll=True)

    def backward(half, t, first, start_row=0, stop_row=1024):
        cols = pl.ds(512 * t, 512)
        if start_row == 0:
            dkvt[...] = jnp.zeros_like(dkvt)

        def step(i, carry):
            rows = pl.ds(pl.multiple_of(i * RB, RB), RB)
            qt = jnp.concatenate([qgt[RB // 128 * i + n] for n in range(RB // 128)], axis=1)
            keys = kv_buf[half, pl.ds(4 * t, 4)].reshape(512, 128)
            dp = dot_nt(gz[rows, :], keys)
            p = wexp[half, rows, cols] * inv_buf[rows, 0:1]
            ds = (p * (dp - del_buf[rows, 0:1])).astype(BF)
            part = dot(ds, keys)
            dkvt[0:64, :] += dot(qt[0:64], ds)
            dkvt[64:128, :] += dot(qt[64:128], p.astype(BF))
            if first:
                dq_acc[rows, :] = part
            else:
                dq_acc[rows, :] += part
            return carry

        lax.fori_loop(start_row // RB, stop_row // RB, step, 0)

    def key_grads(u):
        x = dkvt[:, u * 128 : u * 128 + 128].T
        return x * jnp.where(m128, 0.125, 1.0)

    def sdk_copy(p):
        return rcopy(dkv_x.at[p], dkv_sib.at[p], sdk_s.at[p], sdk_r.at[p], sibling)

    own_piece()
    @pl.when(diag)
    def _():
        pl.semaphore_wait(bar, 21)

    @pl.when(jnp.logical_not(diag))
    def _():
        pl.semaphore_wait(bar, 23)

    gather_far(K)
    gather_far(V)
    make_normed()
    loads[5].wait()
    loads[6].wait()
    for chunk in range(8):
        make_noise(chunk)
    gather_mid(K)
    gather_far(Q)
    make_uq()
    gather_mid(V)
    gather_near(K)
    gather_far(O)
    make_ukv()
    gather_near(V)
    gather_sibling(K)
    gather_mid(Q)
    gather_last(K)
    form_weight(K)
    project_k()
    gather_near(Q)
    gather_sibling(V)
    gather_mid(O)
    gather_last(V)
    form_weight(V)
    project_v()
    a2a_start(M_KV, kv_send, kv_buf.at[0])
    gather_near(O)
    gather_sibling(Q)
    gather_last(Q)
    form_weight(Q)
    project_q()
    a2a_start(M_Q, q_send, q_buf)
    gather_sibling(O)
    forward_kv()
    gather_last(O)
    form_out()
    project_g()
    a2a_start(M_G, g_send, g_buf)
    a2a_start(M_UKV, ukv_send, ukv_buf)
    a2a_start(M_UQ, uq_send, uq_buf)
    ones_kv(0)
    forward_first()
    for p in order:
        skv_copy(p).wait_recv()
    ones_kv(1)
    forward_second()
    finish_forward()
    a2a_start(M_ATT, att_send, att_buf, True)
    a2a_wait_all(M_G, g_send, g_buf)
    unpack_g()
    make_delta()
    for t in range(2):
        backward(1, t, t == 0)
        for u in range(4):
            dkv_x[4 * t + u] = key_grads(u).astype(BF)
            start(sdk_copy(4 * t + u))
    def send_dq(slots):
        for p in slots:
            x = dq_acc[pl.ds(p * 128, 128), :] * 0.125
            dq_send[p] = jnp.where(m64, x[:64], swap(x[64:])).astype(BF)
        a2a_start(M_DQ, dq_send, dq_buf, True, slots)

    def send_dkv(slots):
        for u, p in enumerate(slots):
            sdk_copy(p).wait_recv()
            dkv_send[p] = (key_grads(u) + dkv_sib[p].astype(F32)).astype(BF)
        a2a_start(M_DKV, dkv_send, dkv_buf, True, slots)

    backward(0, 0, False)
    send_dkv(range(4))
    backward(0, 1, False, 0, 512)
    send_dq(range(4))
    backward(0, 1, False, 512, 1024)
    send_dkv(range(4, 8))
    send_dq(range(4, 8))
    a2a_wait_all(M_UKV, ukv_send, ukv_buf)
    a2a_wait_all(M_UQ, uq_send, uq_buf)
    scale_kv = dkv_send[0].astype(F32) * ukv_buf[0].astype(F32)
    scale_q = dq_send[0].astype(F32) * uq_buf[0].astype(F32)
    for p in range(1, 8):
        scale_kv = scale_kv + dkv_send[p].astype(F32) * ukv_buf[p].astype(F32)
        scale_q = scale_q + dq_send[p].astype(F32) * uq_buf[p].astype(F32)
    scale_q = jnp.sum(scale_q, axis=0, keepdims=True)
    scale_q = scale_q + swap(scale_q)
    scale_kv = jnp.sum(scale_kv, axis=0, keepdims=True)
    idx_out[...] = idx_ref[...]
    first_row = lax.broadcasted_iota(jnp.int32, (8, 128), 0) == 0
    ps_buf[0, 0] = jnp.where(first_row, scale_q, scale_kv)

    def ps_copy(stage, k):
        to = (xgroup, ypeer, hpeer)[stage](k)
        return rcopy(ps_buf.at[stage, 0], ps_buf.at[stage, k], ps_s.at[stage, k], ps_r.at[stage, k], to)

    def ps_start(stage):
        for k in (4, 3, 5, 2, 6, 1, 7):
            start(ps_copy(stage, k))

    def ps_wait(stage):
        for k in (1, 7, 2, 6, 3, 5, 4):
            ps_copy(stage, k).wait_recv()

    def ps_sum(stage):
        ps_wait(stage)
        mine = (xl * 4 + xh * 2 + c, y)[stage]
        total = None
        for j in range(8):
            v = ps_buf[stage, (mine + 8 - j) % 8]
            total = v if total is None else total + v
        return total

    ps_start(0)

    def join_pair(a, b):
        a, b = a.astype(F32), b.astype(F32)
        return jnp.concatenate([jnp.where(m64, a, swap(b)), jnp.where(m64, swap(a), b)], 0)

    a2a_wait_all(M_ATT, att_send, att_buf, True)
    att_all = jnp.concatenate(
        [join_pair(att_buf[h], att_buf[h + 1]).astype(BF) for h in range(0, 8, 2)], axis=1
    )
    for t in range(2):
        att_out[:, pl.ds(512 * t, 512)] = dot(att_all, ow[:, pl.ds(512 * t, 512)]).astype(BF)
    ps_buf[1, 0] = ps_sum(0)
    ps_start(1)

    a2a_wait_all(M_DKV, dkv_send, dkv_buf, True)
    dks, dvs = [], []
    for h in range(0, 8, 2):
        a, b = dkv_buf[h].astype(F32), dkv_buf[h + 1].astype(F32)
        dks.append(jnp.where(m128, a, swap(b)))
        dvs.append(jnp.where(m128, swap(a), b))
    gkv = jnp.concatenate(dks + dvs, axis=1).astype(BF)
    grad = [dot_nt(gkv, wbuf[pl.ds(0, 512), HD:])]
    ps_buf[2, 0] = ps_sum(1)
    ps_start(2)
    grad.append(dot_nt(gkv, wbuf[pl.ds(512, 512), HD:]))
    a2a_wait_all(M_DQ, dq_send, dq_buf, True)
    gq = [join_pair(dq_buf[h], dq_buf[h + 1]) for h in range(0, 8, 2)]
    gq = jnp.concatenate(gq, axis=1).astype(BF)
    grad = [grad[t] + dot_nt(gq, wbuf[pl.ds(512 * t, 512), :HD]) for t in range(2)]
    grad = jnp.concatenate(grad, axis=1)
    a = anch[...]
    r = lax.rsqrt(jnp.mean(a * a, axis=-1, keepdims=True) + 1e-06)
    d = grad * gain_ref[...]
    ga = r * (d - a * (r * r * jnp.mean(d * a, axis=-1, keepdims=True)))
    hi = ga.astype(BF)
    hi_out[...] = hi
    lo_out[...] = (ga - hi.astype(F32)).astype(BF)
    ps_wait(2)
    m8 = left_half(8)
    for j in range(4):
        a, b = (ps_buf[2, (z + 8 - h) % 8] for h in (2 * j, 2 * j + 1))
        qk = jnp.where(m8, a, swap(b))
        gs_out[j : j + 1, :] = qk[0:1]
        gs_out[4 + j : 5 + j, :] = qk[1:2]
        gs_out[8 + j : 9 + j, :] = jnp.where(m8, swap(a), b)[1:2]

    for copy in sends:
        copy.wait_send()

    @pl.when(jnp.logical_not(diag))
    def _():
        for msg, src, dst, back in (
            (M_KV, kv_send, kv_buf.at[0], False),
            (M_Q, q_send, q_buf, False),
            (M_G, g_send, g_buf, False),
            (M_UKV, ukv_send, ukv_buf, False),
            (M_UQ, uq_send, uq_buf, False),
            (M_ATT, att_send, att_buf, True),
            (M_DQ, dq_send, dq_buf, True),
            (M_DKV, dkv_send, dkv_buf, True),
        ):
            a2a_one(msg, src, dst, 3, back).wait_send()


def finish(idx_ref, att_ref, hi_ref, lo_ref, gs_ref, att_out, gp_out, gs_out):
    sel_t = (lax.broadcasted_iota(jnp.int32, (PTS, TOK), 0) == idx_ref[...]).astype(BF)
    sel2 = jnp.concatenate([sel_t, sel_t], axis=1)
    for t in range(2):
        cols = pl.ds(512 * t, 512)
        gp_out[:, cols] = dot(sel2, jnp.concatenate([hi_ref[:, cols], lo_ref[:, cols]], axis=0))
    att_out[...] = att_ref[...]
    gs_out[...] = gs_ref[...]


def local(points, anchor_index, norm_gain, weight_mean, weight_scale, noise_seed, out_weight, cotangent):
    vm = pl.BlockSpec(memory_space=pltpu.VMEM)
    hbm = pl.BlockSpec(memory_space=pltpu.HBM)
    V_ = pltpu.VMEM
    dma = pltpu.SemaphoreType.DMA
    att, hi, lo, gs, idx = pl.pallas_call(
        body,
        out_shape=(
            jax.ShapeDtypeStruct((TOK, D), BF),
            jax.ShapeDtypeStruct((TOK, D), BF),
            jax.ShapeDtypeStruct((TOK, D), BF),
            jax.ShapeDtypeStruct((12, 128), F32),
            jax.ShapeDtypeStruct((1, TOK), jnp.int32),
        ),
        in_specs=[hbm] * 8,
        out_specs=(vm, vm, vm, vm, vm),
        scratch_shapes=[
            V_((PTS, D), BF),
            V_((TOK, D), BF),
            V_((1, TOK), jnp.int32),
            V_((1, D), F32),
            V_((32, 3 * HD), BF),
            V_((12, 128), F32),
            V_((12, 128), jnp.int32),
            V_((16, D), BF),
            V_((3, 4, 2, 2, 8, 32, 128), BF),
            V_((4, 2, 2, 8, 16, 256), BF),
            V_((HD, D), BF),
            V_((D, 3 * HD), F32),
            V_((D, 3 * HD), BF),
            V_((D, 3 * HD), BF),
            V_((TOK, D), F32),
            V_((TOK, D), BF),
            V_((TOK, HD), F32),
            V_((8, 128, 128), BF),
            V_((8, 64, 128), BF),
            V_((8, 64, 128), BF),
            V_((8, 128, 128), BF),
            V_((8, 64, 128), BF),
            V_((2, 8, 128, 128), BF),
            V_((2, 8, 128, 128), BF),
            V_((8, 64, 128), BF),
            V_((8, 64, 128), BF),
            V_((8, 128, 128), BF),
            V_((8, 64, 128), BF),
            V_((1024, 128), BF),
            V_((1024, 128), BF),
            V_((8, 128, 128), BF),
            V_((2, 1024, 1024), F32),
            V_((1024, 128), F32),
            V_((1024, 128), F32),
            V_((1024, 128), F32),
            V_((1024, 128), F32),
            V_((128, 512), F32),
            V_((8, 128, 128), BF),
            V_((8, 128, 128), BF),
            V_((8, 128, 128), BF),
            V_((8, 64, 128), BF),
            V_((8, 64, 128), BF),
            V_((8, 64, 128), BF),
            V_((8, 64, 128), BF),
            V_((8, 128, 128), BF),
            V_((3, 8, 8, 128), F32),
            dma((8,)),
            dma((4, 8)),
            dma((4, 8)),
            dma((4,)),
            dma((4,)),
            dma((4, 2, 3)),
            dma((4, 2, 3)),
            dma((4, 5)),
            dma((4, 5)),
            dma((8, 8)),
            dma((8, 8)),
            dma((8,)),
            dma((8,)),
            dma((8,)),
            dma((8,)),
            dma((3, 8)),
            dma((3, 8)),
        ],
        compiler_params=pltpu.CompilerParams(
            collective_id=0, has_side_effects=True, vmem_limit_bytes=44 * 1024 * 1024
        ),
    )(*(
        pltpu.with_memory_space_constraint(x, pltpu.HBM)
        for x in (
            points[0],
            anchor_index,
            norm_gain.reshape(1, D),
            weight_mean,
            weight_scale.reshape(12, 128),
            noise_seed.reshape(12, 128),
            out_weight,
            cotangent[0],
        )
    ))
    att, gpts, gs = pl.pallas_call(
        finish,
        out_shape=(
            jax.ShapeDtypeStruct((TOK, D), BF),
            jax.ShapeDtypeStruct((PTS, D), F32),
            jax.ShapeDtypeStruct((12, 128), F32),
        ),
        in_specs=[vm] * 5,
        out_specs=(vm, vm, vm),
        compiler_params=pltpu.CompilerParams(vmem_limit_bytes=8 * 1024 * 1024),
    )(idx, att, hi, lo, gs)
    return att[None], gpts[None], gs.reshape(3 * HD)


def solution(mesh):
    in_specs = (
        P("outer", "inner", None),
        P("outer", "inner"),
        P(),
        P("outer", None),
        P(),
        P(),
        P("outer", None),
        P("outer", "inner", None),
    )
    out_specs = (P("outer", "inner", None), P("outer", "inner", None), P())
    return jax.shard_map(local, mesh=mesh, in_specs=in_specs, out_specs=out_specs, check_vma=False)
```

```python
import functools

import jax
import jax.numpy as jnp
from jax import lax
from jax.experimental import pallas as pl
from jax.experimental.pallas import tpu as pltpu
from jax.sharding import PartitionSpec as P

MESH = pl.DeviceIdType.MESH
BF = jnp.bfloat16
F32 = jnp.float32

HEADS = 8
TOK = 128
PTS = 256
D = 1024
HD = 512
NZ = 8
NY = 8
LOG2E = 1.4426950408889634

K, V, Q, O = 0, 1, 2, 3
M_KV, M_Q, M_G, M_UKV, M_UQ, M_ATT, M_DQ, M_DKV = range(8)
AWAY = (4, 3, 5, 0, 2, 6, 1, 7)


def left_half(rows):
    return lax.broadcasted_iota(jnp.int32, (rows, 128), 1) < 64


def swap(x):
    return pltpu.roll(x, 64, 1)


def dot(a, b):
    return jnp.dot(a, b, preferred_element_type=F32)


def dot_nt(a, b):
    return lax.dot_general(a, b, (((1,), (1,)), ((), ())), preferred_element_type=F32)


def body(
    points_hbm,
    idx_hbm,
    gain_hbm,
    mean_hbm,
    scale_hbm,
    seed_hbm,
    outw_hbm,
    cot_hbm,
    att_out,
    hi_out,
    lo_out,
    gs_out,
    idx_out,
    pts,
    cot,
    idx_ref,
    gain_ref,
    mean_ref,
    scale_ref,
    seed_ref,
    outw_ref,
    pbuf,
    obuf,
    ow,
    noise_buf,
    nhi,
    wbuf,
    anch,
    normed,
    kproj,
    kv_send,
    q_send,
    g_send,
    ukv_send,
    uq_send,
    kv_buf,
    kv1_buf,
    q_buf,
    g_buf,
    ukv_buf,
    uq_buf,
    qz,
    gz,
    qgt,
    wexp,
    oacc,
    inv_buf,
    del_buf,
    dq_acc,
    dkvt,
    dkv_x,
    dkv_sib,
    dkv_send,
    att_send,
    dq_send,
    att_buf,
    dq_buf,
    dkv_buf,
    ps_buf,
    loc_sem,
    far_s,
    far_r,
    xo_s,
    xo_r,
    near_s,
    near_r,
    sib_s,
    sib_r,
    a2a_s,
    a2a_r,
    skv_s,
    skv_r,
    sdk_s,
    sdk_r,
    ps_s,
    ps_r,
):
    inner = lax.axis_index("inner")
    outer = lax.axis_index("outer")
    z = inner // 2
    xl = inner % 2
    y = outer // 4
    xh = (outer // 2) % 2
    c = outer % 2

    def dev(z_, xl_, y_, xh_, c_):
        return {"inner": z_ * 2 + xl_, "outer": (y_ * 2 + xh_) * 2 + c_}

    def xgroup(k):
        g = (xl * 4 + xh * 2 + c + k) % 8
        return dev(z, g // 4, y, (g // 2) % 2, g % 2)

    def cross(k):
        return dev(z, 1 - xl, (y + k) % NY, 1 - xh, c)

    def zpeer(k):
        return dev((z + k) % NZ, xl, y, xh, c)

    def ypeer(k):
        return dev(z, xl, (y + k) % NY, xh, c)

    def rcopy(src, dst, ssem, rsem, to):
        return pltpu.make_async_remote_copy(
            src_ref=src,
            dst_ref=dst,
            send_sem=ssem,
            recv_sem=rsem,
            device_id=to,
            device_id_type=MESH,
        )

    sends = []

    def start(copy):
        copy.start()
        sends.append(copy)

    loads = [
        pltpu.make_async_copy(a, b, loc_sem.at[n])
        for n, (a, b) in enumerate(
            (
                (mean_hbm, mean_ref),
                (outw_hbm, outw_ref),
                (points_hbm, pts),
                (idx_hbm, idx_ref),
                (gain_hbm, gain_ref),
                (seed_hbm, seed_ref),
                (scale_hbm, scale_ref),
                (cot_hbm, cot),
            )
        )
    ]
    for load in loads:
        load.start()

    diag = xl == c
    bar = pltpu.get_barrier_semaphore()

    def hpeer(k):
        return dev((z + k) % NZ, c, y, xh, xl)

    for k in range(1, 8):
        for to in (ypeer(k), xgroup(k), hpeer(k)):
            pl.semaphore_signal(bar, inc=1, device_id=to, device_id_type=MESH)

    @pl.when(jnp.logical_not(diag))
    def _():
        for k in (1, 7):
            pl.semaphore_signal(bar, inc=1, device_id=zpeer(k), device_id_type=MESH)

    colour = (z + 2 * ((xl + xh) % 2)) % 4
    sibling = dev(z, xl, y, xh, 1 - c)
    across = dev(z, 1 - xl, y, 1 - xh, c)
    near = (zpeer(1), zpeer(7), dev(z, 1 - xl, y, xh, c))
    near_add = (3, 1, 2)

    def piece(part, k, core):
        if part == O:
            return obuf.at[k, core]
        return pbuf.at[part, k, core]

    def own_piece():
        loads[0].wait()
        loads[1].wait()
        for part, base in ((K, HD), (V, 2 * HD), (Q, 0)):
            cols = pl.ds(pl.multiple_of(base + colour * 128, 128), 128)
            pbuf[part, colour, c, xh, y] = mean_ref[:, cols]
        cols = pl.ds(pl.multiple_of(colour * 256, 128), 256)
        obuf[colour, c, xh, y] = outw_ref[:, cols]

    def far_copy(part, k, at):
        b = piece(part, colour, c).at[xh, at]
        return rcopy(b, b, far_s.at[part, k], far_r.at[part, k], ypeer(k))

    def gather_far(part):
        for k in (4, 3, 5, 2, 6, 1, 7):
            start(far_copy(part, k, y))

    def half_out(part, r):
        b = piece(part, colour, c).at[(xh + r) % 2]
        for n, to in enumerate(near):
            start(rcopy(b, b, near_s.at[part, r, n], near_r.at[part, r, n], to))
        start(rcopy(b, b, sib_s.at[part, r], sib_r.at[part, r], sibling))

    def gather_mid(part):
        for k in (1, 7, 2, 6, 3, 5, 4):
            far_copy(part, k, (y + 8 - k) % NY).wait_recv()
        b = piece(part, colour, c).at[xh]
        start(rcopy(b, b, xo_s.at[part], xo_r.at[part], across))
        half_out(part, 0)

    def gather_near(part):
        b = piece(part, colour, c).at[1 - xh]
        rcopy(b, b, xo_s.at[part], xo_r.at[part], across).wait_recv()
        half_out(part, 1)

    def sib_copy(part, n, core):
        b = piece(part, (colour + near_add[n]) % 4, core)
        return rcopy(b, b, sib_s.at[part, 2 + n], sib_r.at[part, 2 + n], sibling)

    def gather_sibling(part):
        for n in range(3):
            for r in range(2):
                b = piece(part, (colour + near_add[n]) % 4, c).at[(xh + r) % 2]
                rcopy(b, b, near_s.at[part, r, n], near_r.at[part, r, n], near[n]).wait_recv()
            start(sib_copy(part, n, c))

    def gather_last(part):
        for r in range(2):
            b = piece(part, colour, 1 - c).at[(xh + r) % 2]
            rcopy(b, b, sib_s.at[part, r], sib_r.at[part, r], sibling).wait_recv()
        for n in range(3):
            sib_copy(part, n, 1 - c).wait_recv()

    def make_normed():
        for load in loads[2:5]:
            load.wait()
        sel_t = (
            lax.broadcasted_iota(jnp.int32, (PTS, TOK), 0) == idx_ref[...]
        ).astype(F32)
        a = dot(sel_t.T.astype(BF), pts[...])
        anch[...] = a
        r = lax.rsqrt(jnp.mean(a * a, axis=-1, keepdims=True) + 1e-06)
        normed[...] = (a * r * gain_ref[...]).astype(BF)

    def row_of(ref, col):
        r0 = col // 128
        return jnp.concatenate([ref[r : r + 1, :] for r in range(r0, r0 + 4)], axis=1)

    def make_noise(chunk):
        def step(t, carry):
            row = pl.multiple_of(chunk * 128 + t * 16, 16)
            for col in range(0, 3 * HD, HD):
                cols = pl.ds(col, HD)
                ids = lax.broadcasted_iota(jnp.int32, (16, HD), 0) + row
                h = row_of(seed_ref, col) * 747796405 + 12345 + ids * 1103515245
                h = h ^ lax.shift_right_logical(h, jnp.full_like(h, 15))
                h = h * 277803737
                h = h ^ lax.shift_right_logical(h, jnp.full_like(h, 16))
                h = lax.shift_right_logical(h, jnp.full_like(h, 8)) & 65535
                n = (h.astype(F32) - 32767.5) * (3.4641016 / 65536.0)
                noise_buf[pl.ds(row, 16), cols] = n
                nhi[pl.ds(row, 16), cols] = n.astype(BF)
            return carry

        lax.fori_loop(0, 8, step, 0)

    def rnd(x):
        return x.astype(BF).astype(F32)

    m128 = left_half(128)
    m64 = left_half(64)

    def form_weight(part):
        col = {K: HD, V: 2 * HD, Q: 0}[part]

        def step(s_, carry):
            scale = row_of(scale_ref, col)
            for half, core in ((0, 0), (0, 1), (1, 0), (1, 1)):
                row = pl.multiple_of(s_ * 128 + half * 64 + core * 32, 32)
                for k in range(4):
                    cols = pl.ds(col + 128 * k, 128)
                    w = pbuf[part, k, core, half, s_].astype(F32) + scale[:, 128 * k : 128 * k + 128] * noise_buf[pl.ds(row, 32), cols]
                    wbuf[pl.ds(row, 32), cols] = w.astype(BF)
            return carry

        lax.fori_loop(0, 8, step, 0)

    def form_out():
        def step(s_, carry):
            for half, core in ((0, 0), (0, 1), (1, 0), (1, 1)):
                row = pl.multiple_of(s_ * 64 + half * 32 + core * 16, 16)
                for k in range(4):
                    ow[pl.ds(row, 16), pl.ds(256 * k, 256)] = obuf[k, core, half, s_]
            return carry

        lax.fori_loop(0, 8, step, 0)

    def pack_kv(k2, v2, h0, ref):
        for u in range(2):
            k = k2[:, u * 128 : u * 128 + 128]
            v = v2[:, u * 128 : u * 128 + 128]
            h = h0 + 2 * u
            ref[h] = jnp.where(m128, k, swap(v)).astype(BF)
            ref[h + 1] = jnp.where(m128, swap(k), v).astype(BF)

    def project_k():
        x = normed[...]
        for t in range(2):
            kproj[:, pl.ds(256 * t, 256)] = rnd(dot(x, wbuf[:, pl.ds(HD + 256 * t, 256)]))

    def project_v():
        x = normed[...]
        for t in range(2):
            v2 = rnd(dot(x, wbuf[:, pl.ds(2 * HD + 256 * t, 256)]))
            pack_kv(kproj[:, pl.ds(256 * t, 256)], v2, 4 * t, kv_send)

    def pack_pair(x, h, ref):
        top, bot = x[:64], x[64:]
        ref[h] = jnp.where(m64, top, swap(bot)).astype(BF)
        ref[h + 1] = jnp.where(m64, swap(top), bot).astype(BF)

    def pack_quad(x, t, ref):
        for u in range(2):
            pack_pair(x[:, u * 128 : u * 128 + 128], 4 * t + 2 * u, ref)

    def project_q():
        x = normed[...]
        for t in range(2):
            pack_quad(rnd(dot(x, wbuf[:, pl.ds(256 * t, 256)])), t, q_send)

    def make_ukv():
        x = normed[...]
        for t in range(2):
            k2 = dot(x, nhi[:, pl.ds(HD + 256 * t, 256)])
            v2 = dot(x, nhi[:, pl.ds(2 * HD + 256 * t, 256)])
            pack_kv(k2, v2, 4 * t, ukv_send)

    def make_uq():
        x = normed[...]
        for t in range(2):
            pack_quad(dot(x, nhi[:, pl.ds(256 * t, 256)]), t, uq_send)

    def project_g():
        loads[7].wait()
        x = cot[...]
        for t in range(2):
            pack_quad(rnd(dot_nt(x, ow[pl.ds(256 * t, 256), :])), t, g_send)

    def a2a_one(msg, src_buf, dst_buf, p, back):
        k = AWAY[p]
        if back:
            src, dst, to = src_buf.at[p], dst_buf.at[z], hpeer(8 - k)
        else:
            src, dst, to = src_buf.at[(z + k) % NZ], dst_buf.at[p], hpeer(k)
        return rcopy(src, dst, a2a_s.at[msg, p], a2a_r.at[msg, p], to)

    def a2a_start(msg, src_buf, dst_buf, back=False, slots=range(8)):
        for p in slots:
            if AWAY[p]:
                start(a2a_one(msg, src_buf, dst_buf, p, back))
                continue

            @pl.when(diag)
            def _():
                if back:
                    dst_buf[z] = src_buf[p]
                else:
                    dst_buf[p] = src_buf[z]

            @pl.when(jnp.logical_not(diag))
            def _():
                a2a_one(msg, src_buf, dst_buf, p, back).start()

    def a2a_wait(msg, src_buf, dst_buf, p, back=False):
        k = AWAY[p]

        def wait():
            dst = dst_buf.at[(z + k) % NZ] if back else dst_buf.at[p]
            src = src_buf.at[0]
            rcopy(src, dst, a2a_s.at[msg, p], a2a_r.at[msg, p], hpeer(k)).wait_recv()

        if k == 0:
            pl.when(jnp.logical_not(diag))(wait)
        else:
            wait()

    order = (3, 6, 7, 4, 5, 1, 2, 0)

    def a2a_wait_all(msg, src_buf, dst_buf, back=False):
        for p in order:
            a2a_wait(msg, src_buf, dst_buf, p, back)

    def skv_copy(p):
        return rcopy(kv_buf.at[0, p], kv_buf.at[1, p], skv_s.at[p], skv_r.at[p], sibling)

    def forward_kv():
        for p in order:
            a2a_wait(M_KV, kv_send, kv_buf.at[0], p)
            start(skv_copy(p))

    def ones_kv(half):
        def step(b, carry):
            kv1_buf[half, b] = jnp.where(m128, 1.0, kv_buf[half, b].astype(F32)).astype(BF)
            return carry

        lax.fori_loop(0, 8, step, 0, unroll=True)

    def unpack_q(b):
        p = q_buf[b].astype(F32)
        zero = jnp.zeros_like(p)
        full = jnp.concatenate([jnp.where(m64, p, zero), jnp.where(m64, swap(p), zero)], 0)
        qz[pl.ds(b * 128, 128), :] = full.astype(BF)

    def unpack_g():
        def step(b, carry):
            p = g_buf[b].astype(F32)
            zero = jnp.zeros_like(p)
            full = jnp.concatenate([jnp.where(m64, zero, swap(p)), jnp.where(m64, zero, p)], 0)
            rows = pl.ds(pl.multiple_of(b * 128, 128), 128)
            gz[rows, :] = full.astype(BF)
            both = full + qz[rows, :].astype(F32)
            qgt[b] = both.T.astype(BF)
            return carry

        lax.fori_loop(0, 8, step, 0, unroll=True)

    RB = 512

    def forward_rows(half, i, first):
        rows = pl.ds(pl.multiple_of(i * RB, RB), RB)
        q = qz[rows, :]
        total = None
        for t in range(2):
            keys = kv_buf[half, pl.ds(4 * t, 4)].reshape(512, 128)
            s = dot_nt(q, keys)
            w = jnp.exp2(s * (0.125 * LOG2E))
            wexp[half, rows, pl.ds(512 * t, 512)] = w
            vals = kv1_buf[half, pl.ds(4 * t, 4)].reshape(512, 128)
            part = dot(w.astype(BF), vals)
            total = part if total is None else total + part
        if first:
            oacc[rows, :] = total
        else:
            oacc[rows, :] += total

    def forward_first():
        for p in order:
            a2a_wait(M_Q, q_send, q_buf, p)
        for p in range(8):
            unpack_q(p)

        def step(i, carry):
            forward_rows(0, i, True)
            return carry

        lax.fori_loop(0, 1024 // RB, step, 0)

    def forward_second():
        def step(i, carry):
            forward_rows(1, i, False)
            return carry

        lax.fori_loop(0, 1024 // RB, step, 0)

    def finish_forward():
        def step(b, carry):
            rows = pl.ds(pl.multiple_of(b * 128, 128), 128)
            o = oacc[rows, :]
            sw = swap(o)
            att = rnd(jnp.where(m128, 0.0, o / jnp.where(m128, 1.0, sw)))
            tot = jnp.where(m128, o, sw)
            inv_buf[rows, :] = 1.0 / tot
            att_send[b] = jnp.where(m64, swap(att[:64]), att[64:]).astype(BF)
            oacc[rows, :] = att
            return carry

        lax.fori_loop(0, 8, step, 0, unroll=True)

    def make_delta():
        def step(b, carry):
            rows = pl.ds(pl.multiple_of(b * 128, 128), 128)
            d = jnp.sum(oacc[rows, :] * gz[rows, :].astype(F32), axis=-1, keepdims=True)
            del_buf[rows, :] = jnp.broadcast_to(d, (128, 128))
            return carry

        lax.fori_loop(0, 8, step, 0, unroll=True)

    def backward(half, t, first, start_row=0, stop_row=1024):
        cols = pl.ds(512 * t, 512)
        if start_row == 0:
            dkvt[...] = jnp.zeros_like(dkvt)

        def step(i, carry):
            rows = pl.ds(pl.multiple_of(i * RB, RB), RB)
            qt = jnp.concatenate([qgt[RB // 128 * i + n] for n in range(RB // 128)], axis=1)
            keys = kv_buf[half, pl.ds(4 * t, 4)].reshape(512, 128)
            dp = dot_nt(gz[rows, :], keys)
            p = wexp[half, rows, cols] * inv_buf[rows, 0:1]
            ds = (p * (dp - del_buf[rows, 0:1])).astype(BF)
            part = dot(ds, keys)
            dkvt[0:64, :] += dot(qt[0:64], ds)
            dkvt[64:128, :] += dot(qt[64:128], p.astype(BF))
            if first:
                dq_acc[rows, :] = part
            else:
                dq_acc[rows, :] += part
            return carry

        lax.fori_loop(start_row // RB, stop_row // RB, step, 0)

    def key_grads(u):
        x = dkvt[:, u * 128 : u * 128 + 128].T
        return x * jnp.where(m128, 0.125, 1.0)

    def sdk_copy(p):
        return rcopy(dkv_x.at[p], dkv_sib.at[p], sdk_s.at[p], sdk_r.at[p], sibling)

    own_piece()
    @pl.when(diag)
    def _():
        pl.semaphore_wait(bar, 21)

    @pl.when(jnp.logical_not(diag))
    def _():
        pl.semaphore_wait(bar, 23)

    gather_far(K)
    gather_far(V)
    make_normed()
    loads[5].wait()
    loads[6].wait()
    for chunk in range(8):
        make_noise(chunk)
    gather_mid(K)
    gather_far(Q)
    make_uq()
    gather_mid(V)
    gather_near(K)
    gather_far(O)
    make_ukv()
    gather_near(V)
    gather_sibling(K)
    gather_mid(Q)
    gather_last(K)
    form_weight(K)
    project_k()
    gather_near(Q)
    gather_sibling(V)
    gather_mid(O)
    gather_last(V)
    form_weight(V)
    project_v()
    a2a_start(M_KV, kv_send, kv_buf.at[0])
    gather_near(O)
    gather_sibling(Q)
    gather_last(Q)
    form_weight(Q)
    project_q()
    a2a_start(M_Q, q_send, q_buf)
    gather_sibling(O)
    forward_kv()
    gather_last(O)
    form_out()
    project_g()
    a2a_start(M_G, g_send, g_buf)
    a2a_start(M_UKV, ukv_send, ukv_buf)
    a2a_start(M_UQ, uq_send, uq_buf)
    ones_kv(0)
    forward_first()
    for p in order:
        skv_copy(p).wait_recv()
    ones_kv(1)
    forward_second()
    finish_forward()
    a2a_start(M_ATT, att_send, att_buf, True)
    a2a_wait_all(M_G, g_send, g_buf)
    unpack_g()
    make_delta()
    for t in range(2):
        backward(1, t, t == 0)
        for u in range(4):
            dkv_x[4 * t + u] = key_grads(u).astype(BF)
            start(sdk_copy(4 * t + u))
    def send_dq(slots):
        for p in slots:
            x = dq_acc[pl.ds(p * 128, 128), :] * 0.125
            dq_send[p] = jnp.where(m64, x[:64], swap(x[64:])).astype(BF)
        a2a_start(M_DQ, dq_send, dq_buf, True, slots)

    def send_dkv(slots):
        for u, p in enumerate(slots):
            sdk_copy(p).wait_recv()
            dkv_send[p] = (key_grads(u) + dkv_sib[p].astype(F32)).astype(BF)
        a2a_start(M_DKV, dkv_send, dkv_buf, True, slots)

    early = len(sends)
    backward(0, 0, False)
    send_dkv(range(4))
    backward(0, 1, False, 0, 512)
    send_dq(range(4))
    backward(0, 1, False, 512, 1024)
    send_dkv(range(4, 8))
    send_dq(range(4, 8))
    a2a_wait_all(M_UKV, ukv_send, ukv_buf)
    a2a_wait_all(M_UQ, uq_send, uq_buf)
    scale_kv = dkv_send[0].astype(F32) * ukv_buf[0].astype(F32)
    scale_q = dq_send[0].astype(F32) * uq_buf[0].astype(F32)
    for p in range(1, 8):
        scale_kv = scale_kv + dkv_send[p].astype(F32) * ukv_buf[p].astype(F32)
        scale_q = scale_q + dq_send[p].astype(F32) * uq_buf[p].astype(F32)
    scale_q = jnp.sum(scale_q, axis=0, keepdims=True)
    scale_q = scale_q + swap(scale_q)
    scale_kv = jnp.sum(scale_kv, axis=0, keepdims=True)
    idx_out[...] = idx_ref[...]
    first_row = lax.broadcasted_iota(jnp.int32, (8, 128), 0) == 0
    ps_buf[0, 0] = jnp.where(first_row, scale_q, scale_kv)

    def ps_copy(stage, k):
        to = (xgroup, ypeer, hpeer)[stage](k)
        return rcopy(ps_buf.at[stage, 0], ps_buf.at[stage, k], ps_s.at[stage, k], ps_r.at[stage, k], to)

    def ps_start(stage):
        for k in (4, 3, 5, 2, 6, 1, 7):
            start(ps_copy(stage, k))

    def ps_wait(stage):
        for k in (1, 7, 2, 6, 3, 5, 4):
            ps_copy(stage, k).wait_recv()

    def ps_sum(stage):
        ps_wait(stage)
        mine = (xl * 4 + xh * 2 + c, y)[stage]
        total = None
        for j in range(8):
            v = ps_buf[stage, (mine + 8 - j) % 8]
            total = v if total is None else total + v
        return total

    ps_start(0)

    for copy in sends[:early]:
        copy.wait_send()
    last_sends = sends[early:]

    def join_pair(a, b):
        a, b = a.astype(F32), b.astype(F32)
        return jnp.concatenate([jnp.where(m64, a, swap(b)), jnp.where(m64, swap(a), b)], 0)

    a2a_wait_all(M_ATT, att_send, att_buf, True)
    att_all = jnp.concatenate(
        [join_pair(att_buf[h], att_buf[h + 1]).astype(BF) for h in range(0, 8, 2)], axis=1
    )
    for t in range(2):
        att_out[:, pl.ds(512 * t, 512)] = dot(att_all, ow[:, pl.ds(512 * t, 512)]).astype(BF)
    ps_buf[1, 0] = ps_sum(0)
    ps_start(1)

    a2a_wait_all(M_DKV, dkv_send, dkv_buf, True)
    dks, dvs = [], []
    for h in range(0, 8, 2):
        a, b = dkv_buf[h].astype(F32), dkv_buf[h + 1].astype(F32)
        dks.append(jnp.where(m128, a, swap(b)))
        dvs.append(jnp.where(m128, swap(a), b))
    gkv = jnp.concatenate(dks + dvs, axis=1).astype(BF)
    grad = [dot_nt(gkv, wbuf[pl.ds(0, 512), HD:])]
    ps_buf[2, 0] = ps_sum(1)
    ps_start(2)
    grad.append(dot_nt(gkv, wbuf[pl.ds(512, 512), HD:]))
    a2a_wait_all(M_DQ, dq_send, dq_buf, True)
    gq = [join_pair(dq_buf[h], dq_buf[h + 1]) for h in range(0, 8, 2)]
    gq = jnp.concatenate(gq, axis=1).astype(BF)
    grad = [grad[t] + dot_nt(gq, wbuf[pl.ds(512 * t, 512), :HD]) for t in range(2)]
    grad = jnp.concatenate(grad, axis=1)
    a = anch[...]
    r = lax.rsqrt(jnp.mean(a * a, axis=-1, keepdims=True) + 1e-06)
    d = grad * gain_ref[...]
    ga = r * (d - a * (r * r * jnp.mean(d * a, axis=-1, keepdims=True)))
    hi = ga.astype(BF)
    hi_out[...] = hi
    lo_out[...] = (ga - hi.astype(F32)).astype(BF)
    ps_wait(2)
    m8 = left_half(8)
    for j in range(4):
        a, b = (ps_buf[2, (z + 8 - h) % 8] for h in (2 * j, 2 * j + 1))
        qk = jnp.where(m8, a, swap(b))
        gs_out[j : j + 1, :] = qk[0:1]
        gs_out[4 + j : 5 + j, :] = qk[1:2]
        gs_out[8 + j : 9 + j, :] = jnp.where(m8, swap(a), b)[1:2]

    for copy in last_sends + sends[early + len(last_sends) :]:
        copy.wait_send()

    @pl.when(jnp.logical_not(diag))
    def _():
        for msg, src, dst, back in (
            (M_KV, kv_send, kv_buf.at[0], False),
            (M_Q, q_send, q_buf, False),
            (M_G, g_send, g_buf, False),
            (M_UKV, ukv_send, ukv_buf, False),
            (M_UQ, uq_send, uq_buf, False),
            (M_ATT, att_send, att_buf, True),
            (M_DQ, dq_send, dq_buf, True),
            (M_DKV, dkv_send, dkv_buf, True),
        ):
            a2a_one(msg, src, dst, 3, back).wait_send()


def finish(idx_ref, att_ref, hi_ref, lo_ref, gs_ref, att_out, gp_out, gs_out):
    sel_t = (lax.broadcasted_iota(jnp.int32, (PTS, TOK), 0) == idx_ref[...]).astype(BF)
    sel2 = jnp.concatenate([sel_t, sel_t], axis=1)
    for t in range(2):
        cols = pl.ds(512 * t, 512)
        gp_out[:, cols] = dot(sel2, jnp.concatenate([hi_ref[:, cols], lo_ref[:, cols]], axis=0))
    att_out[...] = att_ref[...]
    gs_out[...] = gs_ref[...]


def local(points, anchor_index, norm_gain, weight_mean, weight_scale, noise_seed, out_weight, cotangent):
    vm = pl.BlockSpec(memory_space=pltpu.VMEM)
    hbm = pl.BlockSpec(memory_space=pltpu.HBM)
    V_ = pltpu.VMEM
    dma = pltpu.SemaphoreType.DMA
    att, hi, lo, gs, idx = pl.pallas_call(
        body,
        out_shape=(
            jax.ShapeDtypeStruct((TOK, D), BF),
            jax.ShapeDtypeStruct((TOK, D), BF),
            jax.ShapeDtypeStruct((TOK, D), BF),
            jax.ShapeDtypeStruct((12, 128), F32),
            jax.ShapeDtypeStruct((1, TOK), jnp.int32),
        ),
        in_specs=[hbm] * 8,
        out_specs=(vm, vm, vm, vm, vm),
        scratch_shapes=[
            V_((PTS, D), BF),
            V_((TOK, D), BF),
            V_((1, TOK), jnp.int32),
            V_((1, D), F32),
            V_((32, 3 * HD), BF),
            V_((12, 128), F32),
            V_((12, 128), jnp.int32),
            V_((16, D), BF),
            V_((3, 4, 2, 2, 8, 32, 128), BF),
            V_((4, 2, 2, 8, 16, 256), BF),
            V_((HD, D), BF),
            V_((D, 3 * HD), F32),
            V_((D, 3 * HD), BF),
            V_((D, 3 * HD), BF),
            V_((TOK, D), F32),
            V_((TOK, D), BF),
            V_((TOK, HD), F32),
            V_((8, 128, 128), BF),
            V_((8, 64, 128), BF),
            V_((8, 64, 128), BF),
            V_((8, 128, 128), BF),
            V_((8, 64, 128), BF),
            V_((2, 8, 128, 128), BF),
            V_((2, 8, 128, 128), BF),
            V_((8, 64, 128), BF),
            V_((8, 64, 128), BF),
            V_((8, 128, 128), BF),
            V_((8, 64, 128), BF),
            V_((1024, 128), BF),
            V_((1024, 128), BF),
            V_((8, 128, 128), BF),
            V_((2, 1024, 1024), F32),
            V_((1024, 128), F32),
            V_((1024, 128), F32),
            V_((1024, 128), F32),
            V_((1024, 128), F32),
            V_((128, 512), F32),
            V_((8, 128, 128), BF),
            V_((8, 128, 128), BF),
            V_((8, 128, 128), BF),
            V_((8, 64, 128), BF),
            V_((8, 64, 128), BF),
            V_((8, 64, 128), BF),
            V_((8, 64, 128), BF),
            V_((8, 128, 128), BF),
            V_((3, 8, 8, 128), F32),
            dma((8,)),
            dma((4, 8)),
            dma((4, 8)),
            dma((4,)),
            dma((4,)),
            dma((4, 2, 3)),
            dma((4, 2, 3)),
            dma((4, 5)),
            dma((4, 5)),
            dma((8, 8)),
            dma((8, 8)),
            dma((8,)),
            dma((8,)),
            dma((8,)),
            dma((8,)),
            dma((3, 8)),
            dma((3, 8)),
        ],
        compiler_params=pltpu.CompilerParams(
            collective_id=0, has_side_effects=True, vmem_limit_bytes=44 * 1024 * 1024
        ),
    )(*(
        pltpu.with_memory_space_constraint(x, pltpu.HBM)
        for x in (
            points[0],
            anchor_index,
            norm_gain.reshape(1, D),
            weight_mean,
            weight_scale.reshape(12, 128),
            noise_seed.reshape(12, 128),
            out_weight,
            cotangent[0],
        )
    ))
    att, gpts, gs = pl.pallas_call(
        finish,
        out_shape=(
            jax.ShapeDtypeStruct((TOK, D), BF),
            jax.ShapeDtypeStruct((PTS, D), F32),
            jax.ShapeDtypeStruct((12, 128), F32),
        ),
        in_specs=[vm] * 5,
        out_specs=(vm, vm, vm),
        compiler_params=pltpu.CompilerParams(vmem_limit_bytes=8 * 1024 * 1024),
    )(idx, att, hi, lo, gs)
    return att[None], gpts[None], gs.reshape(3 * HD)


def solution(mesh):
    in_specs = (
        P("outer", "inner", None),
        P("outer", "inner"),
        P(),
        P("outer", None),
        P(),
        P(),
        P("outer", None),
        P("outer", "inner", None),
    )
    out_specs = (P("outer", "inner", None), P("outer", "inner", None), P())
    return jax.shard_map(local, mesh=mesh, in_specs=in_specs, out_specs=out_specs, check_vma=False)
```
